128 devices in a mesh: ctx: 16 (over x, y), ch: 8 (over z, core).
Axes of the slice: x: 4, y: 4, z: 4, core: 2. Of those that a mesh axis runs over, the one named last changes fastest.
Arguments:
- pre_gate: bfloat16 [128, 131072], P('ch', 'ctx'), may hold values from -6 to 6
- value: bfloat16 [128, 131072], P('ch', 'ctx'), may hold values from -6 to 6
- post_gate: bfloat16 [128, 131072], P('ch', 'ctx'), may hold values from -6 to 6
- filter_taps: float32 [8, 131072], P('ch', 'ctx'), may hold values from -0.011048543 to 0.011048543, as said below
- skip: float32 [128], P('ch'), may hold values from -6 to 6
Outputs:
- mixed: bfloat16 [128, 131072], P(None, ('ctx', 'ch'))
The draws below stay inside these ranges and needn't reach their ends.
Inputs may be any that keep to these rules, and one draw needn't show every extreme that they name: `filter_taps`: one row of taps for each filter group.
All inputs are finite; a program needn't handle non-finite values.
Results may differ from the reference program's by a relative error of at most 0.013.
Values may be sent and summed in bfloat16 or wider, within the bound.
A program may use at most 128 MiB of HBM per device.

```python
import math
import jax
import jax.numpy as jnp
from jax import lax

C = 128
GROUP = 16
SEQ = 131072
GROUPS = 8


def draw_filter_taps(key, part):
    key = jax.random.fold_in(key, 11)
    tap_scale = 1.0 / math.sqrt(SEQ)
    normal_taps = jax.random.normal(key, (GROUPS, SEQ), jnp.float32)
    return (tap_scale * jnp.clip(normal_taps, -4.0, 4.0)).astype(jnp.float32)


def block_levels(key, extent, cuts, low, largest):
    factor_of = 1.0
    for axis_at, blocks in cuts:
        draws = jax.random.uniform(jax.random.fold_in(jax.random.fold_in(key, 6), axis_at), (blocks,), jnp.float32, low / len(cuts), largest / len(cuts))
        factor_of = factor_of * jnp.repeat(jnp.exp(draws), extent[axis_at] // blocks).reshape((-1,) + (1,) * (len(extent) - 1 - axis_at))
    return factor_of


def scatter_about(own_key, shape, scale, most, shards=(), kind=jnp.bfloat16):
    loudness = block_levels(own_key, shape, shards, -0.22, 0.18) if shards else 1.0
    drawn = jax.random.normal(own_key, shape, jnp.float32) * scale * loudness
    return jnp.minimum(jnp.maximum(drawn, -most), most).astype(kind)


def setup_inputs(seed: int = 0) -> dict:
    seeds = jax.random.split(jax.random.key(seed), 6)
    pre_gate = scatter_about(seeds[0], (C, SEQ), 1.0, 6.0, ((0, 8), (1, 16)))
    value = scatter_about(seeds[1], (C, SEQ), 1.0, 6.0, ((0, 8), (1, 16)))
    post_gate = scatter_about(seeds[2], (C, SEQ), 1.0, 6.0, ((0, 8), (1, 16)))
    filter_taps = draw_filter_taps(jax.random.fold_in(seeds[5], 71), 0)
    skip = scatter_about(seeds[4], (C,), 1.0, 6.0, ((0, 8),), jnp.float32)
    return {"pre_gate": pre_gate, "value": value, "post_gate": post_gate, "filter_taps": filter_taps, "skip": skip}


def reference(pre_gate, value, post_gate, filter_taps, skip):
    fft_length = 2 * SEQ
    signal = (pre_gate.astype(jnp.float32) * value.astype(jnp.float32)).astype(jnp.bfloat16)
    signal_wide = signal.astype(jnp.float32)

    def one_group(items):
        rows_here, taps_here = items
        transformed = jnp.fft.rfft(rows_here, n=fft_length, axis=1)
        filt_spec = jnp.fft.rfft(taps_here, n=fft_length)
        product = transformed * filt_spec[None, :]
        return jnp.fft.irfft(product, n=fft_length, axis=1)[:, :SEQ]

    conv = lax.map(one_group, (signal_wide.reshape(GROUPS, GROUP, SEQ), filter_taps)).reshape(C, SEQ)
    mixed = post_gate.astype(jnp.float32) * (conv + skip[:, None] * signal_wide)
    return mixed.astype(jnp.bfloat16)
```

```python
import jax
import jax.numpy as jnp
import numpy as np
import ml_dtypes
from jax import lax
from jax.experimental import pallas as pl
from jax.experimental.pallas import tpu as pltpu
from jax.sharding import PartitionSpec as P

MESH = pl.DeviceIdType.MESH
F32 = jnp.float32
BF16 = jnp.bfloat16

CTX_X, CTX_Y = 4, 4
CTX = 16
CH = 8
CHANNELS = 16
BLOCK = 8192
R = 256
Q = 512
PIECE = 1024


def build_tables():
    rows = np.arange(R)
    cols = np.arange(Q)
    first = 2 * np.pi * ((np.outer(2 * rows + 1, rows)) % 1024) / 1024.0
    forward = np.concatenate([np.cos(first), -np.sin(first)], axis=0)
    backward = np.concatenate([np.cos(first).T, np.sin(first).T], axis=1) * (2.0**-17)
    turn = 2 * np.pi * np.outer(2 * rows + 1, cols) / 2.0**19
    twiddle = np.stack([np.cos(turn), -np.sin(turn)])
    second = 2 * np.pi * (np.outer(cols, cols) % Q) / Q
    wr, wi = np.cos(second), -np.sin(second)
    table = np.concatenate([np.concatenate([wr, wi], 1), np.concatenate([-wi, wr], 1)], 0)
    half = lambda a: a.astype(np.float32).astype(ml_dtypes.bfloat16)
    return half(forward), half(backward), half(table), twiddle.astype(np.float32)


def kernel(
    pre, val, post, taps, skip, fwd_t, bwd_t, tab_t, tw_t, out,
    pre_v, val_v, taps_v, fwd_v, bwd_v, tab_v, tw_v,
    sig32, tap32, sig_send, tap_send, sig_recv, tap_recv, post_recv,
    spec_b, spec_z, spec_h, back_v, y32, lin32, y_send, y_recv, got32, out_v,
    load_sems, table_sems, sig_sems, tap_sems, post_sems, y_sems, out_sem,
):
    p = lax.axis_index("ctx")
    g = lax.axis_index("ch")

    loads = [
        pltpu.make_async_copy(a, b, load_sems.at[i])
        for i, (a, b) in enumerate([(taps, taps_v), (pre, pre_v), (val, val_v)])
    ]
    for c in loads:
        c.start()

    barrier = pltpu.get_barrier_semaphore()
    px, py = p // CTX_Y, p % CTX_Y
    peers = []
    for dx in (2, 1, 3, 0):
        for dy in (2, 1, 3, 0):
            if dx or dy:
                peers.append(((px + dx) % CTX_X) * CTX_Y + (py + dy) % CTX_Y)
    ch_peers = [(g + j) % CH for j in range(1, CH)]
    for o in peers:
        pl.semaphore_signal(barrier, inc=1, device_id=(o, g), device_id_type=MESH)
    for o in ch_peers:
        pl.semaphore_signal(barrier, inc=1, device_id=(p, o), device_id_type=MESH)

    tables = [
        pltpu.make_async_copy(a, b, table_sems.at[i])
        for i, (a, b) in enumerate(
            [(fwd_t, fwd_v), (tw_t, tw_v), (tab_t, tab_v), (bwd_t, bwd_v)]
        )
    ]
    for c in tables:
        c.start()

    loads[0].wait()
    for r in range(16):
        tap32[r : r + 1, :] = taps_v[0:1, r * Q : (r + 1) * Q]
    tap_send[...] = tap32[...].astype(BF16)
    pl.semaphore_wait(barrier, len(peers) + len(ch_peers))
    for o in peers:
        pltpu.make_async_remote_copy(
            tap_send, tap_recv.at[p], tap_sems.at[0], tap_sems.at[1],
            device_id=(o, g), device_id_type=MESH,
        ).start()
    pltpu.make_async_copy(tap_send, tap_recv.at[p], tap_sems.at[1]).start()

    loads[1].wait()
    loads[2].wait()
    for r in range(16):
        at = pl.ds(r * Q, Q)
        prod = pre_v[:, at].astype(F32) * val_v[:, at].astype(F32)
        for q in range(4):
            sig32[q, pl.ds(r, 16, stride=16), :] = prod[:, q * 128 : (q + 1) * 128]
    for q in range(4):
        sig_send[:, :, q * 128 : (q + 1) * 128] = (
            sig32[q].astype(BF16).reshape(CHANNELS, 16, 128)
        )
    for o in peers:
        pltpu.make_async_remote_copy(
            sig_send.at[o], sig_recv.at[p], sig_sems.at[0], sig_sems.at[1],
            device_id=(o, g), device_id_type=MESH,
        ).start()
    pltpu.make_async_copy(sig_send.at[p], sig_recv.at[p], sig_sems.at[1]).start()

    for o in ch_peers:
        pltpu.make_async_remote_copy(
            post.at[:, pl.ds(pl.multiple_of(o * PIECE, PIECE), PIECE)],
            post_recv.at[g], post_sems.at[0], post_sems.at[1],
            device_id=(p, o), device_id_type=MESH,
        ).start()
    pltpu.make_async_copy(
        post.at[:, pl.ds(pl.multiple_of(g * PIECE, PIECE), PIECE)],
        post_recv.at[g], post_sems.at[1],
    ).start()

    def turned(a_re, a_im):
        t_re, t_im = tw_v[0], tw_v[1]
        return a_re * t_re - a_im * t_im, a_re * t_im + a_im * t_re

    def forward(data):
        a = jnp.dot(fwd_v[...], data, preferred_element_type=F32)
        b_re, b_im = turned(a[:R], a[R:])
        spec_b[:, :Q] = b_re.astype(BF16)
        spec_b[:, Q:] = b_im.astype(BF16)
        return jnp.dot(spec_b[...], tab_v[...], preferred_element_type=F32)

    pltpu.make_async_copy(tap_recv, tap_recv, tap_sems.at[1]).wait()
    for c in tables:
        c.wait()
    spec_h[...] = forward(tap_recv[...].reshape(R, Q))

    pltpu.make_async_copy(sig_recv, sig_recv, sig_sems.at[1]).wait()
    signal = sig_recv[...].reshape(R, Q)
    spec_z[...] = forward(signal)
    z_re, z_im = spec_z[:, :Q], spec_z[:, Q:]
    h_re, h_im = spec_h[:, :Q], spec_h[:, Q:]
    spec_b[:, :Q] = (z_re * h_re - z_im * h_im).astype(BF16)
    spec_b[:, Q:] = (-(z_re * h_im + z_im * h_re)).astype(BF16)
    u = jnp.dot(spec_b[...], tab_v[...], preferred_element_type=F32)
    v_re, v_im = turned(u[:, :Q], u[:, Q:])
    back_v[:R] = v_re.astype(BF16)
    back_v[R:] = v_im.astype(BF16)
    conv = jnp.dot(bwd_v[...], back_v[...], preferred_element_type=F32)
    total = conv + skip[p] * signal.astype(F32)
    for q in range(4):
        y32[q] = total[:, q * 128 : (q + 1) * 128]
    for e in range(2):
        for q in range(4):
            lin32[pl.ds(e * 4 + q, 128, stride=8), :] = y32[q, pl.ds(e, 128, stride=2), :]
    y_send[...] = lin32[...].reshape(128, 8, 128).astype(BF16)

    channel = g * CHANNELS + p
    me = p * CH + g

    def send_piece(k, carry):
        d = lax.rem(me + k, CTX * CH)
        pltpu.make_async_remote_copy(
            y_send.at[d], y_recv.at[channel], y_sems.at[0], y_sems.at[1],
            device_id=(d // CH, lax.rem(d, CH)), device_id_type=MESH,
        ).start()
        return carry

    lax.fori_loop(1, CTX * CH, send_piece, 0)
    pltpu.make_async_copy(y_send.at[me], y_recv.at[channel], y_sems.at[1]).start()

    pltpu.make_async_copy(post_recv, post_recv, post_sems.at[1]).wait()
    pltpu.make_async_copy(y_recv, y_recv, y_sems.at[1]).wait()
    got32[...] = y_recv[...].astype(F32).reshape(CTX * CH * 8, 128)
    for s in range(8):
        at = pl.ds(s * 128, 128)
        gate = post_recv[:, :, at].astype(F32).reshape(128, 128)
        out_v[:, at] = (got32[pl.ds(s, 128, stride=8), :] * gate).astype(BF16)
    done = pltpu.make_async_copy(out_v, out, out_sem)
    done.start()

    tail = pl.ds(0, CTX - 1)
    pltpu.make_async_copy(tap_recv.at[tail], tap_recv.at[tail], tap_sems.at[0]).wait()
    pltpu.make_async_copy(sig_send.at[tail], sig_send.at[tail], sig_sems.at[0]).wait()
    tail = pl.ds(0, CH - 1)
    pltpu.make_async_copy(post_recv.at[tail], post_recv.at[tail], post_sems.at[0]).wait()
    tail = pl.ds(0, CTX * CH - 1)
    pltpu.make_async_copy(y_send.at[tail], y_send.at[tail], y_sems.at[0]).wait()
    done.wait()


def body(pre_gate, value, post_gate, filter_taps, skip):
    fwd_t, bwd_t, tab_t, tw_t = (jnp.asarray(t) for t in build_tables())
    anyspace = pl.BlockSpec(memory_space=pl.ANY)
    vmem = pltpu.VMEM
    return pl.pallas_call(
        kernel,
        out_shape=jax.ShapeDtypeStruct((CTX * CH, PIECE), BF16),
        in_specs=[anyspace] * 4 + [pl.BlockSpec(memory_space=pltpu.SMEM)] + [anyspace] * 4,
        out_specs=anyspace,
        scratch_shapes=[
            vmem((CHANNELS, BLOCK), BF16),
            vmem((CHANNELS, BLOCK), BF16),
            vmem((1, BLOCK), F32),
            vmem((2 * R, R), BF16),
            vmem((R, 2 * R), BF16),
            vmem((2 * Q, 2 * Q), BF16),
            vmem((2, R, Q), F32),
            vmem((4, R, 128), F32),
            vmem((16, Q), F32),
            vmem((CTX, 16, Q), BF16),
            vmem((16, Q), BF16),
            vmem((CTX, 16, Q), BF16),
            vmem((CTX, 16, Q), BF16),
            vmem((CH, CHANNELS, PIECE), BF16),
            vmem((R, 2 * Q), BF16),
            vmem((R, 2 * Q), F32),
            vmem((R, 2 * Q), F32),
            vmem((2 * R, Q), BF16),
            vmem((4, R, 128), F32),
            vmem((CTX * CH * 8, 128), F32),
            vmem((CTX * CH, 8, 128), BF16),
            vmem((CTX * CH, 8, 128), BF16),
            vmem((CTX * CH * 8, 128), F32),
            vmem((CTX * CH, PIECE), BF16),
            pltpu.SemaphoreType.DMA((3,)),
            pltpu.SemaphoreType.DMA((4,)),
            pltpu.SemaphoreType.DMA((2,)),
            pltpu.SemaphoreType.DMA((2,)),
            pltpu.SemaphoreType.DMA((2,)),
            pltpu.SemaphoreType.DMA((2,)),
            pltpu.SemaphoreType.DMA,
        ],
        compiler_params=pltpu.CompilerParams(
            collective_id=0, has_side_effects=True, vmem_limit_bytes=56 * 1024 * 1024
        ),
        name="hyena",
    )(pre_gate, value, post_gate, filter_taps, skip, fwd_t, bwd_t, tab_t, tw_t)


def solution(mesh):
    placed = (P("ch", "ctx"), P("ch", "ctx"), P("ch", "ctx"), P("ch", "ctx"), P("ch"))
    return jax.shard_map(
        body, mesh=mesh, in_specs=placed, out_specs=P(None, ("ctx", "ch")), check_vma=False
    )
```

```python
import jax
import jax.numpy as jnp
import numpy as np
import ml_dtypes
from jax import lax
from jax.experimental import pallas as pl
from jax.experimental.pallas import tpu as pltpu
from jax.sharding import PartitionSpec as P

MESH = pl.DeviceIdType.MESH
F32 = jnp.float32
BF16 = jnp.bfloat16

CTX_Y = 4
CTX = 16
CH = 8
HALF = 8
CHANNELS = 16
BLOCK = 8192
R = 256
Q = 512
PIECE = 1024


def ring(step):
    return min(step, 4 - step)


FAR_FIRST = sorted(
    [
        (dx, dy, dz, dc)
        for dx in range(4)
        for dy in range(4)
        for dz in range(4)
        for dc in range(2)
        if dx or dy or dz or dc
    ],
    key=lambda o: -(ring(o[0]) + ring(o[1]) + ring(o[2])),
)


def build_tables():
    rows = np.arange(R)
    cols = np.arange(Q)
    first = 2 * np.pi * ((np.outer(2 * rows + 1, rows)) % 1024) / 1024.0
    forward = np.concatenate([np.cos(first), -np.sin(first)], axis=0)
    backward = np.concatenate([np.cos(first).T, np.sin(first).T], axis=1) * (2.0**-17)
    turn = 2 * np.pi * np.outer(2 * rows + 1, cols) / 2.0**19
    twiddle = np.stack([np.cos(turn), -np.sin(turn)])
    second = 2 * np.pi * (np.outer(cols, cols) % Q) / Q
    wr, wi = np.cos(second), -np.sin(second)
    table = np.concatenate([np.concatenate([wr, wi], 1), np.concatenate([-wi, wr], 1)], 0)
    half = lambda a: a.astype(np.float32).astype(ml_dtypes.bfloat16)
    return half(forward), half(backward), half(table), twiddle.astype(np.float32)


def kernel(
    pre, val, post, taps, skip_hbm, fwd_t, bwd_t, tab_t, tw_t, y_out, post_out,
    pre_v, val_v, taps_v, fwd_v, bwd_v, tab_v, tw_v,
    sig32, tap32, sig_send, tap_send, sig_recv, tap_recv, skip_send, skip_recv,
    spec_b, spec_z, spec_h, back_v, y32, lin32, y_send,
    skip, load_sems, table_sems, sig_sems, tap_sems, pass_sems, skip_sems, post_sems, y_sems,
):
    p = lax.axis_index("ctx")
    g = lax.axis_index("ch")
    px, py = p // CTX_Y, p % CTX_Y
    z, core = g // 2, g % 2
    xs = [(px + i) % 4 for i in range(4)]
    ys = [(py + i) % 4 for i in range(4)]
    zs = [(z + i) % 4 for i in range(4)]
    cs = [core, 1 - core]
    sibling = z * 2 + 1 - core
    half = p // HALF
    at_home = half == core
    own_group = z * 2 + half
    own_channel = (p % HALF) * 2 + core

    near_x = 2 * core + lax.rem(px, 2)
    flip_x = 2 * core + 1 - lax.rem(px, 2)
    first_x = jnp.where(at_home, flip_x, near_x)
    last_x = jnp.where(at_home, near_x, flip_x)
    workers = [
        first_x * CTX_Y + ys[2], first_x * CTX_Y + ys[1], first_x * CTX_Y + ys[3], last_x * CTX_Y + ys[2],
        last_x * CTX_Y + ys[1], last_x * CTX_Y + ys[3], first_x * CTX_Y + ys[0], last_x * CTX_Y + ys[0],
    ]

    barrier = pltpu.get_barrier_semaphore()
    for dx in (2, 1, 3, 0):
        for dy in (2, 1, 3, 0):
            if dx or dy:
                pl.semaphore_signal(
                    barrier, inc=1, device_id=(xs[dx] * CTX_Y + ys[dy], z * 2 + half), device_id_type=MESH
                )
    for dz, dc in ((2, 0), (2, 1), (1, 0), (3, 0), (1, 1), (3, 1), (0, 1)):
        pl.semaphore_signal(barrier, inc=1, device_id=(p, zs[dz] * 2 + cs[dc]), device_id_type=MESH)

    loads = [
        pltpu.make_async_copy(a, b, load_sems.at[i])
        for i, (a, b) in enumerate([(taps, taps_v), (pre, pre_v), (val, val_v), (skip_hbm, skip)])
    ]
    tables = [
        pltpu.make_async_copy(a, b, table_sems.at[i])
        for i, (a, b) in enumerate([(fwd_t, fwd_v), (tw_t, tw_v), (tab_t, tab_v), (bwd_t, bwd_v)])
    ]
    for c in loads + tables:
        c.start()

    loads[0].wait()
    for r in range(16):
        tap32[r : r + 1, :] = taps_v[0:1, r * Q : (r + 1) * Q]
    tap_send[...] = tap32[...].astype(BF16)
    loads[1].wait()
    loads[2].wait()
    for r in range(16):
        at = pl.ds(r * Q, Q)
        prod = pre_v[:, at].astype(F32) * val_v[:, at].astype(F32)
        for q in range(4):
            sig32[q, pl.ds(r, 16, stride=16), :] = prod[:, q * 128 : (q + 1) * 128]
    for q in range(4):
        sig_send[:, :, q * 128 : (q + 1) * 128] = (
            sig32[q].astype(BF16).reshape(CHANNELS, 16, 128)
        )

    @pl.when(at_home)
    def _():
        pl.semaphore_wait(barrier, 7 + 14)

    @pl.when(jnp.logical_not(at_home))
    def _():
        pl.semaphore_wait(barrier, 7 + 16)

    def send_taps(o):
        pltpu.make_async_remote_copy(
            tap_send, tap_recv.at[p], tap_sems.at[0], tap_sems.at[1],
            device_id=(o, z * 2 + half), device_id_type=MESH,
        ).start()

    def send_signal(o, k):
        pltpu.make_async_remote_copy(
            sig_send.at[lax.rem(o, HALF) * 2 + k], sig_recv.at[p], sig_sems.at[0], sig_sems.at[1],
            device_id=(o, z * 2 + k), device_id_type=MESH,
        ).start()

    for o in workers[:-1]:
        send_taps(o)
    for o in workers[:-1]:
        send_signal(o, 0)
        send_signal(o, 1)
    far = workers[-1]

    @pl.when(at_home)
    def _():
        pltpu.make_async_copy(tap_send, tap_recv.at[p], tap_sems.at[1]).start()
        pltpu.make_async_remote_copy(
            sig_send.at[lax.rem(p, HALF) * 2 + 1 - core], sig_recv.at[p], sig_sems.at[0], sig_sems.at[1],
            device_id=(p, sibling), device_id_type=MESH,
        ).start()
        pltpu.make_async_copy(sig_send.at[own_channel], sig_recv.at[p], sig_sems.at[1]).start()

    @pl.when(jnp.logical_not(at_home))
    def _():
        send_taps(far)
        send_signal(far, 0)
        send_signal(far, 1)

    loads[3].wait()
    skip_send[...] = jnp.full((8, 128), skip[(p % HALF) * 2 + 1 - core], F32)
    to_sibling = pltpu.make_async_remote_copy(
        skip_send, skip_recv, skip_sems.at[0], skip_sems.at[1],
        device_id=(p, sibling), device_id_type=MESH,
    )
    to_sibling.start()

    def post_part(o):
        return post.at[:, pl.ds(pl.multiple_of(o * PIECE, PIECE), PIECE)]

    for dz, dc in ((2, 0), (2, 1), (1, 0), (3, 0), (1, 1), (3, 1), (0, 1)):
        o = zs[dz] * 2 + cs[dc]
        pltpu.make_async_remote_copy(
            post_part(o), post_out.at[g], post_sems.at[0], post_sems.at[1],
            device_id=(p, o), device_id_type=MESH,
        ).start()
    pltpu.make_async_copy(post_part(g), post_out.at[g], post_sems.at[1]).start()

    mine = tap_recv.at[pl.ds(core * HALF, HALF)]
    theirs = tap_recv.at[pl.ds((1 - core) * HALF, HALF)]
    pltpu.make_async_copy(mine, mine, tap_sems.at[1]).wait()
    passed = pltpu.make_async_remote_copy(
        mine, mine, pass_sems.at[0], pass_sems.at[1], device_id=(p, sibling), device_id_type=MESH
    )
    passed.start()

    def turned(a_re, a_im):
        t_re, t_im = tw_v[0], tw_v[1]
        return a_re * t_re - a_im * t_im, a_re * t_im + a_im * t_re

    def forward(data):
        a = jnp.dot(fwd_v[...], data, preferred_element_type=F32)
        b_re, b_im = turned(a[:R], a[R:])
        spec_b[:, :Q] = b_re.astype(BF16)
        spec_b[:, Q:] = b_im.astype(BF16)
        return jnp.dot(spec_b[...], tab_v[...], preferred_element_type=F32)

    for c in tables:
        c.wait()
    pltpu.make_async_copy(theirs, theirs, pass_sems.at[1]).wait()
    spec_h[...] = forward(tap_recv[...].reshape(R, Q))

    pltpu.make_async_copy(sig_recv, sig_recv, sig_sems.at[1]).wait()
    signal = sig_recv[...].reshape(R, Q)
    spec_z[...] = forward(signal)
    z_re, z_im = spec_z[:, :Q], spec_z[:, Q:]
    h_re, h_im = spec_h[:, :Q], spec_h[:, Q:]
    spec_b[:, :Q] = (z_re * h_re - z_im * h_im).astype(BF16)
    spec_b[:, Q:] = (-(z_re * h_im + z_im * h_re)).astype(BF16)
    u = jnp.dot(spec_b[...], tab_v[...], preferred_element_type=F32)
    v_re, v_im = turned(u[:, :Q], u[:, Q:])
    back_v[:R] = v_re.astype(BF16)
    back_v[R:] = v_im.astype(BF16)
    conv = jnp.dot(bwd_v[...], back_v[...], preferred_element_type=F32)
    to_sibling.wait_recv()
    weight = jnp.where(at_home, skip[own_channel], skip_recv[0:1, :])
    for q in range(4):
        at = slice(q * 128, (q + 1) * 128)
        y32[q] = conv[:, at] + weight * signal[:, at].astype(F32)
    for e in range(2):
        for q in range(4):
            lin32[pl.ds(e * 4 + q, 128, stride=8), :] = y32[q, pl.ds(e, 128, stride=2), :]
    y_send[...] = lin32[...].reshape(CTX * CH, 8, 128).astype(BF16)

    channel = own_group * CHANNELS + own_channel
    for dx, dy, dz, dc in FAR_FIRST:
        o_ctx = xs[dx] * CTX_Y + ys[dy]
        o_ch = zs[dz] * 2 + cs[dc]
        pltpu.make_async_remote_copy(
            y_send.at[o_ctx * CH + o_ch], y_out.at[channel], y_sems.at[0], y_sems.at[1],
            device_id=(o_ctx, o_ch), device_id_type=MESH,
        ).start()
    pltpu.make_async_copy(y_send.at[p * CH + g], y_out.at[channel], y_sems.at[1]).start()

    @pl.when(at_home)
    def _():
        part = sig_send.at[pl.ds(0, 15)]
        pltpu.make_async_copy(part, part, sig_sems.at[0]).wait()
        part = tap_recv.at[pl.ds(0, 7)]
        pltpu.make_async_copy(part, part, tap_sems.at[0]).wait()

    @pl.when(jnp.logical_not(at_home))
    def _():
        pltpu.make_async_copy(sig_send, sig_send, sig_sems.at[0]).wait()
        part = tap_recv.at[pl.ds(0, 8)]
        pltpu.make_async_copy(part, part, tap_sems.at[0]).wait()

    passed.wait_send()
    to_sibling.wait_send()
    part = post_out.at[pl.ds(0, CH - 1)]
    pltpu.make_async_copy(part, part, post_sems.at[0]).wait()
    pltpu.make_async_copy(post_out, post_out, post_sems.at[1]).wait()
    part = y_send.at[pl.ds(0, CTX * CH - 1)]
    pltpu.make_async_copy(part, part, y_sems.at[0]).wait()
    pltpu.make_async_copy(y_out, y_out, y_sems.at[1]).wait()


def gate_kernel(y, post, out, wide):
    wide[...] = y[...].astype(F32).reshape(wide.shape)
    rows = out.shape[0]
    for s in range(8):
        at = pl.ds(s * 128, 128)
        gate = post[:, at].astype(F32)
        out[:, at] = (wide[pl.ds(s, rows, stride=8), :] * gate).astype(BF16)


def body(pre_gate, value, post_gate, filter_taps, skip):
    fwd_t, bwd_t, tab_t, tw_t = (jnp.asarray(t) for t in build_tables())
    anyspace = pl.BlockSpec(memory_space=pl.ANY)
    vmem = pltpu.VMEM
    dma = pltpu.SemaphoreType.DMA
    whole = pl.BlockSpec(memory_space=vmem)
    conv, gate = pl.pallas_call(
        kernel,
        out_shape=[
            vmem((CTX * CH, 8, 128), BF16),
            vmem((CH, CHANNELS, PIECE), BF16),
        ],
        in_specs=[anyspace] * 9,
        out_specs=[whole, whole],
        scratch_shapes=[
            vmem((CHANNELS, BLOCK), BF16),
            vmem((CHANNELS, BLOCK), BF16),
            vmem((1, BLOCK), F32),
            vmem((2 * R, R), BF16),
            vmem((R, 2 * R), BF16),
            vmem((2 * Q, 2 * Q), BF16),
            vmem((2, R, Q), F32),
            vmem((4, R, 128), F32),
            vmem((16, Q), F32),
            vmem((CTX, 16, Q), BF16),
            vmem((16, Q), BF16),
            vmem((CTX, 16, Q), BF16),
            vmem((CTX, 16, Q), BF16),
            vmem((8, 128), F32),
            vmem((8, 128), F32),
            vmem((R, 2 * Q), BF16),
            vmem((R, 2 * Q), F32),
            vmem((R, 2 * Q), F32),
            vmem((2 * R, Q), BF16),
            vmem((4, R, 128), F32),
            vmem((CTX * CH * 8, 128), F32),
            vmem((CTX * CH, 8, 128), BF16),
            pltpu.SMEM((16,), F32),
            dma((4,)),
            dma((4,)),
            dma((2,)),
            dma((2,)),
            dma((2,)),
            dma((2,)),
            dma((2,)),
            dma((2,)),
        ],
        compiler_params=pltpu.CompilerParams(
            collective_id=0, has_side_effects=True, vmem_limit_bytes=56 * 1024 * 1024
        ),
        name="hyena",
    )(pre_gate, value, post_gate, filter_taps, skip, fwd_t, bwd_t, tab_t, tw_t)
    return pl.pallas_call(
        gate_kernel,
        out_shape=jax.ShapeDtypeStruct((CTX * CH, PIECE), BF16),
        in_specs=[whole, whole],
        out_specs=whole,
        scratch_shapes=[vmem((CTX * CH * 8, 128), F32)],
        compiler_params=pltpu.CompilerParams(vmem_limit_bytes=4 * 1024 * 1024),
        name="gate",
    )(conv, gate.reshape(CTX * CH, PIECE))


def solution(mesh):
    placed = (P("ch", "ctx"), P("ch", "ctx"), P("ch", "ctx"), P("ch", "ctx"), P("ch"))
    return jax.shard_map(
        body, mesh=mesh, in_specs=placed, out_specs=P(None, ("ctx", "ch")), check_vma=False
    )
```

```python
import jax
import jax.numpy as jnp
import numpy as np
import ml_dtypes
from jax import lax
from jax.experimental import pallas as pl
from jax.experimental.pallas import tpu as pltpu
from jax.sharding import PartitionSpec as P

MESH = pl.DeviceIdType.MESH
F32 = jnp.float32
BF16 = jnp.bfloat16

CTX_Y = 4
CTX = 16
CH = 8
HALF = 8
CHANNELS = 16
BLOCK = 8192
R = 256
Q = 512
PIECE = 1024


def ring(step):
    return min(step, 4 - step)


FAR_FIRST = sorted(
    [
        (dx, dy, dz, dc)
        for dx in range(4)
        for dy in range(4)
        for dz in range(4)
        for dc in range(2)
        if dx or dy or dz or dc
    ],
    key=lambda o: -(ring(o[0]) + ring(o[1]) + ring(o[2])),
)


def pair(table, flip):
    re, im = table.real, table.imag
    return np.block([[re, im], [im, -re]]) if flip else np.block([[re, im], [-im, re]])


def build_tables():
    rows = np.arange(R)
    cols = np.arange(Q)
    part = np.arange(128)
    first = 2 * np.pi * ((np.outer(2 * rows + 1, rows)) % 1024) / 1024.0
    forward = np.concatenate([np.cos(first), -np.sin(first)], axis=0)
    order = np.concatenate([rows[0::2], rows[1::2]])
    backward = np.concatenate([np.cos(first).T, np.sin(first).T], axis=1)[order] * (2.0**-17)
    turn = 2 * np.pi * np.outer(2 * rows + 1, cols) / 2.0**19
    twiddle = np.stack([np.cos(turn), -np.sin(turn)])
    waves = [np.exp(-2j * np.pi * (np.outer(part, d + 4 * part) % Q) / Q) for d in range(4)]
    there = np.concatenate([pair(w, False) for w in waves], axis=0)
    back = np.concatenate([pair(w.T, True) for w in waves], axis=0)
    half = lambda a: a.astype(np.float32).astype(ml_dtypes.bfloat16)
    return half(forward), half(backward), half(there), half(back), twiddle.astype(np.float32)


def times(a, b):
    return a[0] * b[0] - a[1] * b[1], a[0] * b[1] + a[1] * b[0]


def four_point(v):
    (r0, i0), (r1, i1), (r2, i2), (r3, i3) = v
    sr, si, dr, di = r0 + r2, i0 + i2, r0 - r2, i0 - i2
    ur, ui, er, ei = r1 + r3, i1 + i3, r1 - r3, i1 - i3
    return [(sr + ur, si + ui), (dr + ei, di - er), (sr - ur, si - ui), (dr - ei, di + er)]


def kernel(
    pre, val, post, taps, skip_hbm, fwd_t, bwd_t, there_t, back_t, tw_t, y_out, post_out,
    pre_v, val_v, taps_v, fwd_v, bwd_v, there_v, back_v, tw_v,
    sig32, tap32, sig_send, tap_send, sig_recv, tap_recv, skip_send, skip_recv,
    spec_h, y32, lin32, y_send,
    skip, load_sems, table_sems, sig_sems, tap_sems, pass_sems, skip_sems, post_sems, y_sems,
):
    p = lax.axis_index("ctx")
    g = lax.axis_index("ch")
    px, py = p // CTX_Y, p % CTX_Y
    z, core = g // 2, g % 2
    xs = [(px + i) % 4 for i in range(4)]
    ys = [(py + i) % 4 for i in range(4)]
    zs = [(z + i) % 4 for i in range(4)]
    cs = [core, 1 - core]
    sibling = z * 2 + 1 - core
    half = p // HALF
    at_home = half == core
    own_group = z * 2 + half
    own_channel = (p % HALF) * 2 + core

    near_x = 2 * core + lax.rem(px, 2)
    flip_x = 2 * core + 1 - lax.rem(px, 2)
    first_x = jnp.where(at_home, flip_x, near_x)
    last_x = jnp.where(at_home, near_x, flip_x)
    workers = [
        first_x * CTX_Y + ys[2], first_x * CTX_Y + ys[1], first_x * CTX_Y + ys[3], last_x * CTX_Y + ys[2],
        last_x * CTX_Y + ys[1], last_x * CTX_Y + ys[3], first_x * CTX_Y + ys[0], last_x * CTX_Y + ys[0],
    ]

    barrier = pltpu.get_barrier_semaphore()
    for dx in (2, 1, 3, 0):
        for dy in (2, 1, 3, 0):
            if dx or dy:
                pl.semaphore_signal(
                    barrier, inc=1, device_id=(xs[dx] * CTX_Y + ys[dy], z * 2 + half), device_id_type=MESH
                )
    for dz, dc in ((2, 0), (2, 1), (1, 0), (3, 0), (1, 1), (3, 1), (0, 1)):
        pl.semaphore_signal(barrier, inc=1, device_id=(p, zs[dz] * 2 + cs[dc]), device_id_type=MESH)

    loads = [
        pltpu.make_async_copy(a, b, load_sems.at[i])
        for i, (a, b) in enumerate([(taps, taps_v), (pre, pre_v), (val, val_v), (skip_hbm, skip)])
    ]
    tables = [
        pltpu.make_async_copy(a, b, table_sems.at[i])
        for i, (a, b) in enumerate([(fwd_t, fwd_v), (tw_t, tw_v), (there_t, there_v), (back_t, back_v), (bwd_t, bwd_v)])
    ]
    for c in loads + tables:
        c.start()

    loads[0].wait()
    for r in range(16):
        tap32[r : r + 1, :] = taps_v[0:1, r * Q : (r + 1) * Q]
    tap_send[...] = tap32[...].astype(BF16)
    loads[1].wait()
    loads[2].wait()
    for r in range(16):
        at = pl.ds(r * Q, Q)
        prod = pre_v[:, at].astype(F32) * val_v[:, at].astype(F32)
        for q in range(4):
            sig32[q, pl.ds(r, 16, stride=16), :] = prod[:, q * 128 : (q + 1) * 128]
    for q in range(4):
        sig_send[:, :, q * 128 : (q + 1) * 128] = (
            sig32[q].astype(BF16).reshape(CHANNELS, 16, 128)
        )

    @pl.when(at_home)
    def _():
        pl.semaphore_wait(barrier, 7 + 14)

    @pl.when(jnp.logical_not(at_home))
    def _():
        pl.semaphore_wait(barrier, 7 + 16)

    def send_taps(o):
        pltpu.make_async_remote_copy(
            tap_send, tap_recv.at[p], tap_sems.at[0], tap_sems.at[1],
            device_id=(o, z * 2 + half), device_id_type=MESH,
        ).start()

    def send_signal(o, k):
        pltpu.make_async_remote_copy(
            sig_send.at[lax.rem(o, HALF) * 2 + k], sig_recv.at[p], sig_sems.at[0], sig_sems.at[1],
            device_id=(o, z * 2 + k), device_id_type=MESH,
        ).start()

    for o in workers[:-1]:
        send_taps(o)
    for o in workers[:-1]:
        send_signal(o, 0)
        send_signal(o, 1)
    far = workers[-1]

    @pl.when(at_home)
    def _():
        pltpu.make_async_copy(tap_send, tap_recv.at[p], tap_sems.at[1]).start()
        pltpu.make_async_remote_copy(
            sig_send.at[lax.rem(p, HALF) * 2 + 1 - core], sig_recv.at[p], sig_sems.at[0], sig_sems.at[1],
            device_id=(p, sibling), device_id_type=MESH,
        ).start()
        pltpu.make_async_copy(sig_send.at[own_channel], sig_recv.at[p], sig_sems.at[1]).start()

    @pl.when(jnp.logical_not(at_home))
    def _():
        send_taps(far)
        send_signal(far, 0)
        send_signal(far, 1)

    loads[3].wait()
    skip_send[...] = jnp.full((8, 128), skip[(p % HALF) * 2 + 1 - core], F32)
    to_sibling = pltpu.make_async_remote_copy(
        skip_send, skip_recv, skip_sems.at[0], skip_sems.at[1],
        device_id=(p, sibling), device_id_type=MESH,
    )
    to_sibling.start()

    def post_part(o):
        return post.at[:, pl.ds(pl.multiple_of(o * PIECE, PIECE), PIECE)]

    for dz, dc in ((2, 0), (2, 1), (1, 0), (3, 0), (1, 1), (3, 1), (0, 1)):
        o = zs[dz] * 2 + cs[dc]
        pltpu.make_async_remote_copy(
            post_part(o), post_out.at[g], post_sems.at[0], post_sems.at[1],
            device_id=(p, o), device_id_type=MESH,
        ).start()
    pltpu.make_async_copy(post_part(g), post_out.at[g], post_sems.at[1]).start()

    mine = tap_recv.at[pl.ds(core * HALF, HALF)]
    theirs = tap_recv.at[pl.ds((1 - core) * HALF, HALF)]
    pltpu.make_async_copy(mine, mine, tap_sems.at[1]).wait()
    passed = pltpu.make_async_remote_copy(
        mine, mine, pass_sems.at[0], pass_sems.at[1], device_id=(p, sibling), device_id_type=MESH
    )
    passed.start()

    def lanes(a):
        return slice(a * 128, (a + 1) * 128)

    def turn(a):
        return tw_v[0, :, lanes(a)], tw_v[1, :, lanes(a)]

    def joined(re, im):
        return jnp.concatenate([re.astype(BF16), im.astype(BF16)], axis=1)

    def spectrum(data):
        a = jnp.dot(fwd_v[...], data, preferred_element_type=F32)
        parts = four_point([times((a[:R, lanes(i)], a[R:, lanes(i)]), turn(i)) for i in range(4)])
        return [
            jnp.dot(joined(*parts[d]), there_v[d * R : (d + 1) * R, :], preferred_element_type=F32)
            for d in range(4)
        ]

    for c in tables:
        c.wait()
    pltpu.make_async_copy(theirs, theirs, pass_sems.at[1]).wait()
    for d, part in enumerate(spectrum(tap_recv[...].reshape(R, Q))):
        spec_h[d] = part

    pltpu.make_async_copy(sig_recv, sig_recv, sig_sems.at[1]).wait()
    signal = sig_recv[...].reshape(R, Q)
    to_sibling.wait_recv()
    weight = jnp.where(at_home, skip[own_channel], skip_recv[0:1, :])
    for q in range(4):
        y32[q] = weight * signal[:, lanes(q)].astype(F32)
    parts = []
    for d, part in enumerate(spectrum(signal)):
        prod = times((part[:, :128], part[:, 128:]), (spec_h[d, :, :128], spec_h[d, :, 128:]))
        part = jnp.dot(joined(*prod), back_v[d * R : (d + 1) * R, :], preferred_element_type=F32)
        parts.append((part[:, :128], part[:, 128:]))
    parts = [times(part, turn(i)) for i, part in enumerate(four_point(parts))]
    columns = jnp.concatenate(
        [jnp.concatenate([part[i].astype(BF16) for part in parts], axis=1) for i in range(2)], axis=0
    )
    conv = jnp.dot(bwd_v[...], columns, preferred_element_type=F32)
    for e in range(2):
        for q in range(4):
            lin32[pl.ds(e * 4 + q, 128, stride=8), :] = (
                conv[e * 128 : (e + 1) * 128, lanes(q)] + y32[q, pl.ds(e, 128, stride=2), :]
            )
    y_send[...] = lin32[...].reshape(CTX * CH, 8, 128).astype(BF16)

    channel = own_group * CHANNELS + own_channel
    for dx, dy, dz, dc in FAR_FIRST:
        o_ctx = xs[dx] * CTX_Y + ys[dy]
        o_ch = zs[dz] * 2 + cs[dc]
        pltpu.make_async_remote_copy(
            y_send.at[o_ctx * CH + o_ch], y_out.at[channel], y_sems.at[0], y_sems.at[1],
            device_id=(o_ctx, o_ch), device_id_type=MESH,
        ).start()
    pltpu.make_async_copy(y_send.at[p * CH + g], y_out.at[channel], y_sems.at[1]).start()

    @pl.when(at_home)
    def _():
        part = sig_send.at[pl.ds(0, 15)]
        pltpu.make_async_copy(part, part, sig_sems.at[0]).wait()
        part = tap_recv.at[pl.ds(0, 7)]
        pltpu.make_async_copy(part, part, tap_sems.at[0]).wait()

    @pl.when(jnp.logical_not(at_home))
    def _():
        pltpu.make_async_copy(sig_send, sig_send, sig_sems.at[0]).wait()
        part = tap_recv.at[pl.ds(0, 8)]
        pltpu.make_async_copy(part, part, tap_sems.at[0]).wait()

    passed.wait_send()
    to_sibling.wait_send()
    part = post_out.at[pl.ds(0, CH - 1)]
    pltpu.make_async_copy(part, part, post_sems.at[0]).wait()
    pltpu.make_async_copy(post_out, post_out, post_sems.at[1]).wait()
    part = y_send.at[pl.ds(0, CTX * CH - 1)]
    pltpu.make_async_copy(part, part, y_sems.at[0]).wait()
    pltpu.make_async_copy(y_out, y_out, y_sems.at[1]).wait()


def gate_kernel(y, post, out, wide):
    wide[...] = y[...].astype(F32).reshape(wide.shape)
    rows = out.shape[0]
    for s in range(8):
        at = pl.ds(s * 128, 128)
        gate = post[:, at].astype(F32)
        out[:, at] = (wide[pl.ds(s, rows, stride=8), :] * gate).astype(BF16)


def body(pre_gate, value, post_gate, filter_taps, skip):
    tables = tuple(jnp.asarray(t) for t in build_tables())
    anyspace = pl.BlockSpec(memory_space=pl.ANY)
    vmem = pltpu.VMEM
    dma = pltpu.SemaphoreType.DMA
    whole = pl.BlockSpec(memory_space=vmem)
    conv, gate = pl.pallas_call(
        kernel,
        out_shape=[
            vmem((CTX * CH, 8, 128), BF16),
            vmem((CH, CHANNELS, PIECE), BF16),
        ],
        in_specs=[anyspace] * 10,
        out_specs=[whole, whole],
        scratch_shapes=[
            vmem((CHANNELS, BLOCK), BF16),
            vmem((CHANNELS, BLOCK), BF16),
            vmem((1, BLOCK), F32),
            vmem((2 * R, R), BF16),
            vmem((R, 2 * R), BF16),
            vmem((4 * R, R), BF16),
            vmem((4 * R, R), BF16),
            vmem((2, R, Q), F32),
            vmem((4, R, 128), F32),
            vmem((16, Q), F32),
            vmem((CTX, 16, Q), BF16),
            vmem((16, Q), BF16),
            vmem((CTX, 16, Q), BF16),
            vmem((CTX, 16, Q), BF16),
            vmem((8, 128), F32),
            vmem((8, 128), F32),
            vmem((4, R, 2 * 128), F32),
            vmem((4, R, 128), F32),
            vmem((CTX * CH * 8, 128), F32),
            vmem((CTX * CH, 8, 128), BF16),
            pltpu.SMEM((16,), F32),
            dma((4,)),
            dma((5,)),
            dma((2,)),
            dma((2,)),
            dma((2,)),
            dma((2,)),
            dma((2,)),
            dma((2,)),
        ],
        compiler_params=pltpu.CompilerParams(
            collective_id=0, has_side_effects=True, vmem_limit_bytes=56 * 1024 * 1024
        ),
        name="hyena",
    )(pre_gate, value, post_gate, filter_taps, skip, *tables)
    return pl.pallas_call(
        gate_kernel,
        out_shape=jax.ShapeDtypeStruct((CTX * CH, PIECE), BF16),
        in_specs=[whole, whole],
        out_specs=whole,
        scratch_shapes=[vmem((CTX * CH * 8, 128), F32)],
        compiler_params=pltpu.CompilerParams(vmem_limit_bytes=4 * 1024 * 1024),
        name="gate",
    )(conv, gate.reshape(CTX * CH, PIECE))


def solution(mesh):
    placed = (P("ch", "ctx"), P("ch", "ctx"), P("ch", "ctx"), P("ch", "ctx"), P("ch"))
    return jax.shard_map(
        body, mesh=mesh, in_specs=placed, out_specs=P(None, ("ctx", "ch")), check_vma=False
    )
```

```python
import jax
import jax.numpy as jnp
import numpy as np
import ml_dtypes
from jax import lax
from jax.experimental import pallas as pl
from jax.experimental.pallas import tpu as pltpu
from jax.sharding import PartitionSpec as P

MESH = pl.DeviceIdType.MESH
F32 = jnp.float32
BF16 = jnp.bfloat16

CTX_Y = 4
CTX = 16
CH = 8
HALF = 8
CHANNELS = 16
BLOCK = 8192
R = 256
Q = 512
PIECE = 1024


def ring(step):
    return min(step, 4 - step)


FAR_FIRST = sorted(
    [(dx, dy, dz) for dx in range(4) for dy in range(4) for dz in range(4)],
    key=lambda o: -(ring(o[0]) + ring(o[1]) + ring(o[2])),
)


def pair(table, flip):
    re, im = table.real, table.imag
    return np.block([[re, im], [im, -re]]) if flip else np.block([[re, im], [-im, re]])


def build_tables():
    rows = np.arange(R)
    cols = np.arange(Q)
    part = np.arange(128)
    first = 2 * np.pi * ((np.outer(2 * rows + 1, rows)) % 1024) / 1024.0
    forward = np.concatenate([np.cos(first), -np.sin(first)], axis=0)
    order = np.concatenate([rows[0::2], rows[1::2]])
    backward = np.concatenate([np.cos(first).T, np.sin(first).T], axis=1)[order] * (2.0**-17)
    turn = 2 * np.pi * np.outer(2 * rows + 1, cols) / 2.0**19
    twiddle = np.stack([np.cos(turn), -np.sin(turn)])
    waves = [np.exp(-2j * np.pi * (np.outer(part, d + 4 * part) % Q) / Q) for d in range(4)]
    there = np.concatenate([pair(w, False) for w in waves], axis=0)
    back = np.concatenate([pair(w.T, True) for w in waves], axis=0)
    half = lambda a: a.astype(np.float32).astype(ml_dtypes.bfloat16)
    return half(forward), half(backward), half(there), half(back), twiddle.astype(np.float32)


def times(a, b):
    return a[0] * b[0] - a[1] * b[1], a[0] * b[1] + a[1] * b[0]


def four_point(v):
    (r0, i0), (r1, i1), (r2, i2), (r3, i3) = v
    sr, si, dr, di = r0 + r2, i0 + i2, r0 - r2, i0 - i2
    ur, ui, er, ei = r1 + r3, i1 + i3, r1 - r3, i1 - i3
    return [(sr + ur, si + ui), (dr + ei, di - er), (sr - ur, si - ui), (dr - ei, di + er)]


def kernel(
    pre, val, post, taps, skip_hbm, fwd_t, bwd_t, there_t, back_t, tw_t, y_out, post_out,
    pre_v, val_v, taps_v, fwd_v, bwd_v, there_v, back_v, tw_v,
    sig32, tap32, sig_send, tap_send, sig_recv, tap_recv, skip_send, skip_recv,
    spec_h, y32, lin32, y_send,
    skip, load_sems, table_sems, sig_sems, tap_sems, pass_sems, skip_sems, post_sems, y_sems,
):
    p = lax.axis_index("ctx")
    g = lax.axis_index("ch")
    px, py = p // CTX_Y, p % CTX_Y
    z, core = g // 2, g % 2
    xs = [(px + i) % 4 for i in range(4)]
    ys = [(py + i) % 4 for i in range(4)]
    zs = [(z + i) % 4 for i in range(4)]
    cs = [core, 1 - core]
    sibling = z * 2 + 1 - core
    half = p // HALF
    at_home = half == core
    own_group = z * 2 + half
    own_channel = (p % HALF) * 2 + core

    near_x = 2 * core + lax.rem(px, 2)
    flip_x = 2 * core + 1 - lax.rem(px, 2)
    first_x = jnp.where(at_home, flip_x, near_x)
    last_x = jnp.where(at_home, near_x, flip_x)
    workers = [
        first_x * CTX_Y + ys[2], first_x * CTX_Y + ys[1], first_x * CTX_Y + ys[3], last_x * CTX_Y + ys[2],
        last_x * CTX_Y + ys[1], last_x * CTX_Y + ys[3], first_x * CTX_Y + ys[0], last_x * CTX_Y + ys[0],
    ]

    barrier = pltpu.get_barrier_semaphore()
    for dx in (2, 1, 3, 0):
        for dy in (2, 1, 3, 0):
            if dx or dy:
                pl.semaphore_signal(
                    barrier, inc=1, device_id=(xs[dx] * CTX_Y + ys[dy], z * 2 + half), device_id_type=MESH
                )
    for dz, dc in ((2, 0), (2, 1), (1, 0), (3, 0), (1, 1), (3, 1), (0, 1)):
        pl.semaphore_signal(barrier, inc=1, device_id=(p, zs[dz] * 2 + cs[dc]), device_id_type=MESH)

    loads = [
        pltpu.make_async_copy(a, b, load_sems.at[i])
        for i, (a, b) in enumerate([(taps, taps_v), (pre, pre_v), (val, val_v), (skip_hbm, skip)])
    ]
    tables = [
        pltpu.make_async_copy(a, b, table_sems.at[i])
        for i, (a, b) in enumerate([(fwd_t, fwd_v), (tw_t, tw_v), (there_t, there_v), (back_t, back_v), (bwd_t, bwd_v)])
    ]
    for c in loads + tables:
        c.start()

    loads[0].wait()
    for r in range(16):
        tap32[r : r + 1, :] = taps_v[0:1, r * Q : (r + 1) * Q]
    tap_send[...] = tap32[...].astype(BF16)
    loads[1].wait()
    loads[2].wait()
    for r in range(16):
        at = pl.ds(r * Q, Q)
        prod = pre_v[:, at].astype(F32) * val_v[:, at].astype(F32)
        for q in range(4):
            sig32[q, pl.ds(r, 16, stride=16), :] = prod[:, q * 128 : (q + 1) * 128]
    for q in range(4):
        sig_send[:, :, q * 128 : (q + 1) * 128] = (
            sig32[q].astype(BF16).reshape(CHANNELS, 16, 128)
        )

    @pl.when(at_home)
    def _():
        pl.semaphore_wait(barrier, 7 + 14)

    @pl.when(jnp.logical_not(at_home))
    def _():
        pl.semaphore_wait(barrier, 7 + 16)

    def send_taps(o):
        pltpu.make_async_remote_copy(
            tap_send, tap_recv.at[p], tap_sems.at[0], tap_sems.at[1],
            device_id=(o, z * 2 + half), device_id_type=MESH,
        ).start()

    def send_signal(o, k):
        pltpu.make_async_remote_copy(
            sig_send.at[lax.rem(o, HALF) * 2 + k], sig_recv.at[p], sig_sems.at[0], sig_sems.at[1],
            device_id=(o, z * 2 + k), device_id_type=MESH,
        ).start()

    for o in workers[:-1]:
        send_taps(o)
    for o in workers[:-1]:
        send_signal(o, 0)
        send_signal(o, 1)
    far = workers[-1]

    @pl.when(at_home)
    def _():
        pltpu.make_async_copy(tap_send, tap_recv.at[p], tap_sems.at[1]).start()
        pltpu.make_async_remote_copy(
            sig_send.at[lax.rem(p, HALF) * 2 + 1 - core], sig_recv.at[p], sig_sems.at[0], sig_sems.at[1],
            device_id=(p, sibling), device_id_type=MESH,
        ).start()
        pltpu.make_async_copy(sig_send.at[own_channel], sig_recv.at[p], sig_sems.at[1]).start()

    @pl.when(jnp.logical_not(at_home))
    def _():
        send_taps(far)
        send_signal(far, 0)
        send_signal(far, 1)

    loads[3].wait()
    skip_send[...] = jnp.full((8, 128), skip[(p % HALF) * 2 + 1 - core], F32)
    to_sibling = pltpu.make_async_remote_copy(
        skip_send, skip_recv, skip_sems.at[0], skip_sems.at[1],
        device_id=(p, sibling), device_id_type=MESH,
    )
    to_sibling.start()

    def post_part(o):
        return post.at[:, pl.ds(pl.multiple_of(o * PIECE, PIECE), PIECE)]

    for dz, dc in ((2, 0), (2, 1), (1, 0), (3, 0), (1, 1), (3, 1), (0, 1)):
        o = zs[dz] * 2 + cs[dc]
        pltpu.make_async_remote_copy(
            post_part(o), post_out.at[g], post_sems.at[0], post_sems.at[1],
            device_id=(p, o), device_id_type=MESH,
        ).start()
    pltpu.make_async_copy(post_part(g), post_out.at[g], post_sems.at[1]).start()

    mine = tap_recv.at[pl.ds(core * HALF, HALF)]
    theirs = tap_recv.at[pl.ds((1 - core) * HALF, HALF)]
    pltpu.make_async_copy(mine, mine, tap_sems.at[1]).wait()
    passed = pltpu.make_async_remote_copy(
        mine, mine, pass_sems.at[0], pass_sems.at[1], device_id=(p, sibling), device_id_type=MESH
    )
    passed.start()

    def lanes(a):
        return slice(a * 128, (a + 1) * 128)

    def turn(a):
        return tw_v[0, :, lanes(a)], tw_v[1, :, lanes(a)]

    def joined(re, im):
        return jnp.concatenate([re.astype(BF16), im.astype(BF16)], axis=1)

    def spectrum(data):
        a = jnp.dot(fwd_v[...], data, preferred_element_type=F32)
        parts = four_point([times((a[:R, lanes(i)], a[R:, lanes(i)]), turn(i)) for i in range(4)])
        return [
            jnp.dot(joined(*parts[d]), there_v[d * R : (d + 1) * R, :], preferred_element_type=F32)
            for d in range(4)
        ]

    for c in tables:
        c.wait()
    pltpu.make_async_copy(theirs, theirs, pass_sems.at[1]).wait()
    for d, part in enumerate(spectrum(tap_recv[...].reshape(R, Q))):
        spec_h[d] = part

    pltpu.make_async_copy(sig_recv, sig_recv, sig_sems.at[1]).wait()
    signal = sig_recv[...].reshape(R, Q)
    to_sibling.wait_recv()
    weight = jnp.where(at_home, skip[own_channel], skip_recv[0:1, :])
    for q in range(4):
        y32[q] = weight * signal[:, lanes(q)].astype(F32)
    parts = []
    for d, part in enumerate(spectrum(signal)):
        prod = times((part[:, :128], part[:, 128:]), (spec_h[d, :, :128], spec_h[d, :, 128:]))
        part = jnp.dot(joined(*prod), back_v[d * R : (d + 1) * R, :], preferred_element_type=F32)
        parts.append((part[:, :128], part[:, 128:]))
    parts = [times(part, turn(i)) for i, part in enumerate(four_point(parts))]
    columns = jnp.concatenate(
        [jnp.concatenate([part[i].astype(BF16) for part in parts], axis=1) for i in range(2)], axis=0
    )
    conv = jnp.dot(bwd_v[...], columns, preferred_element_type=F32)
    for e in range(2):
        for q in range(4):
            lin32[pl.ds(e * 4 + q, 128, stride=8), :] = (
                conv[e * 128 : (e + 1) * 128, lanes(q)] + y32[q, pl.ds(e, 128, stride=2), :]
            )
    y_send[...] = lin32[...].reshape(CTX * CH, 8, 128).astype(BF16)

    channel = own_group * CHANNELS + own_channel
    def send_piece(o_ctx, o_ch):
        pltpu.make_async_remote_copy(
            y_send.at[o_ctx * CH + o_ch], y_out.at[channel], y_sems.at[0], y_sems.at[1],
            device_id=(o_ctx, o_ch), device_id_type=MESH,
        ).start()

    for o_ch in (1, 0):

        @pl.when(jnp.logical_or(p != 0, g != o_ch))
        def _(o_ch=o_ch):
            send_piece(0, o_ch)

    for dx, dy, dz in FAR_FIRST:
        o_ctx = xs[dx] * CTX_Y + ys[dy]

        @pl.when(o_ctx + zs[dz] != 0)
        def _(o_ctx=o_ctx, dx=dx, dy=dy, dz=dz):
            for dc in (0, 1) if dx or dy or dz else (1,):
                send_piece(o_ctx, zs[dz] * 2 + cs[dc])

    pltpu.make_async_copy(y_send.at[p * CH + g], y_out.at[channel], y_sems.at[1]).start()

    @pl.when(at_home)
    def _():
        part = sig_send.at[pl.ds(0, 15)]
        pltpu.make_async_copy(part, part, sig_sems.at[0]).wait()
        part = tap_recv.at[pl.ds(0, 7)]
        pltpu.make_async_copy(part, part, tap_sems.at[0]).wait()

    @pl.when(jnp.logical_not(at_home))
    def _():
        pltpu.make_async_copy(sig_send, sig_send, sig_sems.at[0]).wait()
        part = tap_recv.at[pl.ds(0, 8)]
        pltpu.make_async_copy(part, part, tap_sems.at[0]).wait()

    passed.wait_send()
    to_sibling.wait_send()
    part = post_out.at[pl.ds(0, CH - 1)]
    pltpu.make_async_copy(part, part, post_sems.at[0]).wait()
    pltpu.make_async_copy(post_out, post_out, post_sems.at[1]).wait()
    part = y_send.at[pl.ds(0, CTX * CH - 1)]
    pltpu.make_async_copy(part, part, y_sems.at[0]).wait()
    pltpu.make_async_copy(y_out, y_out, y_sems.at[1]).wait()


def gate_kernel(y, post, out, wide):
    wide[...] = y[...].astype(F32).reshape(wide.shape)
    rows = out.shape[0]
    for s in range(8):
        at = pl.ds(s * 128, 128)
        gate = post[:, at].astype(F32)
        out[:, at] = (wide[pl.ds(s, rows, stride=8), :] * gate).astype(BF16)


def body(pre_gate, value, post_gate, filter_taps, skip):
    tables = tuple(jnp.asarray(t) for t in build_tables())
    anyspace = pl.BlockSpec(memory_space=pl.ANY)
    vmem = pltpu.VMEM
    dma = pltpu.SemaphoreType.DMA
    whole = pl.BlockSpec(memory_space=vmem)
    conv, gate = pl.pallas_call(
        kernel,
        out_shape=[
            vmem((CTX * CH, 8, 128), BF16),
            vmem((CH, CHANNELS, PIECE), BF16),
        ],
        in_specs=[anyspace] * 10,
        out_specs=[whole, whole],
        scratch_shapes=[
            vmem((CHANNELS, BLOCK), BF16),
            vmem((CHANNELS, BLOCK), BF16),
            vmem((1, BLOCK), F32),
            vmem((2 * R, R), BF16),
            vmem((R, 2 * R), BF16),
            vmem((4 * R, R), BF16),
            vmem((4 * R, R), BF16),
            vmem((2, R, Q), F32),
            vmem((4, R, 128), F32),
            vmem((16, Q), F32),
            vmem((CTX, 16, Q), BF16),
            vmem((16, Q), BF16),
            vmem((CTX, 16, Q), BF16),
            vmem((CTX, 16, Q), BF16),
            vmem((8, 128), F32),
            vmem((8, 128), F32),
            vmem((4, R, 2 * 128), F32),
            vmem((4, R, 128), F32),
            vmem((CTX * CH * 8, 128), F32),
            vmem((CTX * CH, 8, 128), BF16),
            pltpu.SMEM((16,), F32),
            dma((4,)),
            dma((5,)),
            dma((2,)),
            dma((2,)),
            dma((2,)),
            dma((2,)),
            dma((2,)),
            dma((2,)),
        ],
        compiler_params=pltpu.CompilerParams(
            collective_id=0, has_side_effects=True, vmem_limit_bytes=56 * 1024 * 1024
        ),
        name="hyena",
    )(pre_gate, value, post_gate, filter_taps, skip, *tables)
    return pl.pallas_call(
        gate_kernel,
        out_shape=jax.ShapeDtypeStruct((CTX * CH, PIECE), BF16),
        in_specs=[whole, whole],
        out_specs=whole,
        scratch_shapes=[vmem((CTX * CH * 8, 128), F32)],
        compiler_params=pltpu.CompilerParams(vmem_limit_bytes=4 * 1024 * 1024),
        name="gate",
    )(conv, gate.reshape(CTX * CH, PIECE))


def solution(mesh):
    placed = (P("ch", "ctx"), P("ch", "ctx"), P("ch", "ctx"), P("ch", "ctx"), P("ch"))
    return jax.shard_map(
        body, mesh=mesh, in_specs=placed, out_specs=P(None, ("ctx", "ch")), check_vma=False
    )
```

```python
import jax
import jax.numpy as jnp
import numpy as np
import ml_dtypes
from jax import lax
from jax.experimental import pallas as pl
from jax.experimental.pallas import tpu as pltpu
from jax.sharding import PartitionSpec as P

MESH = pl.DeviceIdType.MESH
F32 = jnp.float32
BF16 = jnp.bfloat16

CTX_Y = 4
CTX = 16
CH = 8
HALF = 8
CHANNELS = 16
BLOCK = 8192
R = 256
Q = 512
GATE_PARTS = 4
PIECE = 1024


def ring(step):
    return min(step, 4 - step)


FAR_FIRST = sorted([(dx, dy) for dx in range(4) for dy in range(4)], key=lambda o: -(ring(o[0]) + ring(o[1])))


def pair(table, flip):
    re, im = table.real, table.imag
    return np.block([[re, im], [im, -re]]) if flip else np.block([[re, im], [-im, re]])


def build_tables():
    rows = np.arange(R)
    cols = np.arange(Q)
    part = np.arange(128)
    first = 2 * np.pi * ((np.outer(2 * rows + 1, rows)) % 1024) / 1024.0
    forward = np.concatenate([np.cos(first), -np.sin(first)], axis=0)
    order = np.concatenate([rows[0::2], rows[1::2]])
    backward = np.concatenate([np.cos(first).T, np.sin(first).T], axis=1)[order] * (2.0**-17)
    turn = 2 * np.pi * np.outer(2 * rows + 1, cols) / 2.0**19
    twiddle = np.stack([np.cos(turn), -np.sin(turn)])
    waves = [np.exp(-2j * np.pi * (np.outer(part, d + 4 * part) % Q) / Q) for d in range(4)]
    there = np.concatenate([pair(w, False) for w in waves], axis=0)
    back = np.concatenate([pair(w.T, True) for w in waves], axis=0)
    half = lambda a: a.astype(np.float32).astype(ml_dtypes.bfloat16)
    return half(forward), half(backward), half(there), half(back), twiddle.astype(np.float32)


def times(a, b):
    return a[0] * b[0] - a[1] * b[1], a[0] * b[1] + a[1] * b[0]


def four_point(v):
    (r0, i0), (r1, i1), (r2, i2), (r3, i3) = v
    sr, si, dr, di = r0 + r2, i0 + i2, r0 - r2, i0 - i2
    ur, ui, er, ei = r1 + r3, i1 + i3, r1 - r3, i1 - i3
    return [(sr + ur, si + ui), (dr + ei, di - er), (sr - ur, si - ui), (dr - ei, di + er)]


def kernel(
    pre, val, post, taps, skip_hbm, fwd_t, bwd_t, there_t, back_t, tw_t, y_out, post_out,
    pre_v, val_v, taps_v, fwd_v, bwd_v, there_v, back_v, tw_v,
    sig32, tap32, sig_send, tap_send, sig_recv, tap_recv, skip_send, skip_recv,
    spec_h, y32, lin32, y_send,
    skip, load_sems, table_sems, sig_sems, tap_sems, pass_sems, skip_sems, post_sems, y_sems,
):
    p = lax.axis_index("ctx")
    g = lax.axis_index("ch")
    px, py = p // CTX_Y, p % CTX_Y
    z, core = g // 2, g % 2
    xs = [(px + i) % 4 for i in range(4)]
    ys = [(py + i) % 4 for i in range(4)]
    zs = [(z + i) % 4 for i in range(4)]
    cs = [core, 1 - core]
    sibling = z * 2 + 1 - core
    half = py // 2
    at_home = half == core
    own_group = z * 2 + half
    place = lax.rem(py, 2) * 4 + px
    own_channel = place * 2 + core
    taps_core = p // HALF

    near_y = 2 * core + lax.rem(py, 2)
    flip_y = 2 * core + 1 - lax.rem(py, 2)
    first_y = jnp.where(at_home, flip_y, near_y)
    last_y = jnp.where(at_home, near_y, flip_y)
    workers = [
        (xs[2], first_y), (xs[1], first_y), (xs[3], first_y), (xs[2], last_y),
        (xs[1], last_y), (xs[3], last_y), (xs[0], first_y), (xs[0], last_y),
    ]

    barrier = pltpu.get_barrier_semaphore()
    for dx in (2, 1, 3, 0):
        for dy in (2, 1, 3, 0):
            if dx or dy:
                pl.semaphore_signal(
                    barrier, inc=1, device_id=(xs[dx] * CTX_Y + ys[dy], z * 2 + half), device_id_type=MESH
                )
    for dz, dc in ((2, 0), (2, 1), (1, 0), (3, 0), (1, 1), (3, 1), (0, 1)):
        pl.semaphore_signal(barrier, inc=1, device_id=(p, zs[dz] * 2 + cs[dc]), device_id_type=MESH)

    loads = [
        pltpu.make_async_copy(a, b, load_sems.at[i])
        for i, (a, b) in enumerate([(taps, taps_v), (pre, pre_v), (val, val_v), (skip_hbm, skip)])
    ]
    tables = [
        pltpu.make_async_copy(a, b, table_sems.at[i])
        for i, (a, b) in enumerate([(fwd_t, fwd_v), (tw_t, tw_v), (there_t, there_v), (back_t, back_v), (bwd_t, bwd_v)])
    ]
    for c in loads + tables:
        c.start()

    loads[0].wait()
    for r in range(16):
        tap32[r : r + 1, :] = taps_v[0:1, r * Q : (r + 1) * Q]
    tap_send[...] = tap32[...].astype(BF16)
    loads[1].wait()
    loads[2].wait()
    for r in range(16):
        at = pl.ds(r * Q, Q)
        prod = pre_v[:, at].astype(F32) * val_v[:, at].astype(F32)
        for q in range(4):
            sig32[q, pl.ds(r, 16, stride=16), :] = prod[:, q * 128 : (q + 1) * 128]
    for q in range(4):
        sig_send[:, :, q * 128 : (q + 1) * 128] = (
            sig32[q].astype(BF16).reshape(CHANNELS, 16, 128)
        )

    @pl.when(at_home)
    def _():
        pl.semaphore_wait(barrier, 7 + 14)

    @pl.when(jnp.logical_not(at_home))
    def _():
        pl.semaphore_wait(barrier, 7 + 16)

    def send_taps(o):
        pltpu.make_async_remote_copy(
            tap_send, tap_recv.at[p], tap_sems.at[0], tap_sems.at[1],
            device_id=(o[0] * CTX_Y + o[1], z * 2 + taps_core), device_id_type=MESH,
        ).start()

    def send_signal(o, k):
        pltpu.make_async_remote_copy(
            sig_send.at[(lax.rem(o[1], 2) * 4 + o[0]) * 2 + k], sig_recv.at[p], sig_sems.at[0], sig_sems.at[1],
            device_id=(o[0] * CTX_Y + o[1], z * 2 + k), device_id_type=MESH,
        ).start()

    for o in workers[:-1]:
        send_taps(o)
    for o in workers[:-1]:
        send_signal(o, 0)
        send_signal(o, 1)
    keeps_taps = jnp.logical_and(at_home, taps_core == core)

    @pl.when(keeps_taps)
    def _():
        pltpu.make_async_copy(tap_send, tap_recv.at[p], tap_sems.at[1]).start()

    @pl.when(jnp.logical_not(keeps_taps))
    def _():
        send_taps(workers[-1])

    @pl.when(at_home)
    def _():
        pltpu.make_async_remote_copy(
            sig_send.at[place * 2 + 1 - core], sig_recv.at[p], sig_sems.at[0], sig_sems.at[1],
            device_id=(p, sibling), device_id_type=MESH,
        ).start()
        pltpu.make_async_copy(sig_send.at[own_channel], sig_recv.at[p], sig_sems.at[1]).start()

    @pl.when(jnp.logical_not(at_home))
    def _():
        send_signal(workers[-1], 0)
        send_signal(workers[-1], 1)

    loads[3].wait()
    skip_send[...] = jnp.full((8, 128), skip[place * 2 + 1 - core], F32)
    to_sibling = pltpu.make_async_remote_copy(
        skip_send, skip_recv, skip_sems.at[0], skip_sems.at[1],
        device_id=(p, sibling), device_id_type=MESH,
    )
    to_sibling.start()

    def post_part(o):
        return post.at[:, pl.ds(pl.multiple_of(o * PIECE, PIECE), PIECE)]

    for dz, dc in ((2, 0), (2, 1), (1, 0), (3, 0), (1, 1), (3, 1), (0, 1)):
        o = zs[dz] * 2 + cs[dc]
        pltpu.make_async_remote_copy(
            post_part(o), post_out.at[g], post_sems.at[0], post_sems.at[1],
            device_id=(p, o), device_id_type=MESH,
        ).start()
    pltpu.make_async_copy(post_part(g), post_out.at[g], post_sems.at[1]).start()

    mine = tap_recv.at[pl.ds(core * HALF, HALF)]
    theirs = tap_recv.at[pl.ds((1 - core) * HALF, HALF)]
    pltpu.make_async_copy(mine, mine, tap_sems.at[1]).wait()
    passed = pltpu.make_async_remote_copy(
        mine, mine, pass_sems.at[0], pass_sems.at[1], device_id=(p, sibling), device_id_type=MESH
    )
    passed.start()

    def lanes(a):
        return slice(a * 128, (a + 1) * 128)

    def turn(a):
        return tw_v[0, :, lanes(a)], tw_v[1, :, lanes(a)]

    def joined(re, im):
        return jnp.concatenate([re.astype(BF16), im.astype(BF16)], axis=1)

    def spectrum(data):
        a = jnp.dot(fwd_v[...], data, preferred_element_type=F32)
        parts = four_point([times((a[:R, lanes(i)], a[R:, lanes(i)]), turn(i)) for i in range(4)])
        return [
            jnp.dot(joined(*parts[d]), there_v[d * R : (d + 1) * R, :], preferred_element_type=F32)
            for d in range(4)
        ]

    for c in tables:
        c.wait()
    pltpu.make_async_copy(theirs, theirs, pass_sems.at[1]).wait()
    for d, part in enumerate(spectrum(tap_recv[...].reshape(R, Q))):
        spec_h[d] = part

    pltpu.make_async_copy(sig_recv, sig_recv, sig_sems.at[1]).wait()
    signal = sig_recv[...].reshape(R, Q)
    to_sibling.wait_recv()
    weight = jnp.where(at_home, skip[own_channel], skip_recv[0:1, :])
    for q in range(4):
        y32[q] = weight * signal[:, lanes(q)].astype(F32)
    parts = []
    for d, part in enumerate(spectrum(signal)):
        prod = times((part[:, :128], part[:, 128:]), (spec_h[d, :, :128], spec_h[d, :, 128:]))
        part = jnp.dot(joined(*prod), back_v[d * R : (d + 1) * R, :], preferred_element_type=F32)
        parts.append((part[:, :128], part[:, 128:]))
    parts = [times(part, turn(i)) for i, part in enumerate(four_point(parts))]
    columns = jnp.concatenate(
        [jnp.concatenate([part[i].astype(BF16) for part in parts], axis=1) for i in range(2)], axis=0
    )
    conv = jnp.dot(bwd_v[...], columns, preferred_element_type=F32)
    for e in range(2):
        for q in range(4):
            lin32[pl.ds(e * 4 + q, 128, stride=8), :] = (
                conv[e * 128 : (e + 1) * 128, lanes(q)] + y32[q, pl.ds(e, 128, stride=2), :]
            )
    y_send[...] = lin32[...].reshape(CTX * CH, 8, 128).astype(BF16)

    channel = own_group * CHANNELS + own_channel
    def send_piece(o_ctx, o_ch):
        pltpu.make_async_remote_copy(
            y_send.at[o_ctx * CH + o_ch], y_out.at[channel], y_sems.at[0], y_sems.at[1],
            device_id=(o_ctx, o_ch), device_id_type=MESH,
        ).start()

    for o_ch in (1, 0):

        @pl.when(jnp.logical_or(p != 0, g != o_ch))
        def _(o_ch=o_ch):
            send_piece(0, o_ch)

    for o_z in range(4):
        for dx, dy in FAR_FIRST:
            o_ctx = xs[dx] * CTX_Y + ys[dy]
            for c in range(2):

                @pl.when(jnp.logical_and(o_ctx + o_z != 0, jnp.logical_or(o_ctx != p, o_z * 2 + c != g)))
                def _(o_ctx=o_ctx, o_ch=o_z * 2 + c):
                    send_piece(o_ctx, o_ch)

    pltpu.make_async_copy(y_send.at[p * CH + g], y_out.at[channel], y_sems.at[1]).start()

    @pl.when(at_home)
    def _():
        part = sig_send.at[pl.ds(0, 15)]
        pltpu.make_async_copy(part, part, sig_sems.at[0]).wait()

    @pl.when(jnp.logical_not(at_home))
    def _():
        pltpu.make_async_copy(sig_send, sig_send, sig_sems.at[0]).wait()

    @pl.when(keeps_taps)
    def _():
        part = tap_recv.at[pl.ds(0, 7)]
        pltpu.make_async_copy(part, part, tap_sems.at[0]).wait()

    @pl.when(jnp.logical_not(keeps_taps))
    def _():
        part = tap_recv.at[pl.ds(0, 8)]
        pltpu.make_async_copy(part, part, tap_sems.at[0]).wait()

    passed.wait_send()
    to_sibling.wait_send()
    part = post_out.at[pl.ds(0, CH - 1)]
    pltpu.make_async_copy(part, part, post_sems.at[0]).wait()
    pltpu.make_async_copy(post_out, post_out, post_sems.at[1]).wait()
    part = y_send.at[pl.ds(0, CTX * CH - 1)]
    pltpu.make_async_copy(part, part, y_sems.at[0]).wait()
    pltpu.make_async_copy(y_out, y_out, y_sems.at[1]).wait()


def gate_kernel(y, post, out, wide, made, sems):
    rows = CTX * CH // GATE_PARTS
    copies = []
    for k in range(GATE_PARTS):
        own = pl.ds(k * rows, rows)
        wide[k] = y[own].astype(F32).reshape(rows * 8, 128)
        for s in range(8):
            at = pl.ds(s * 128, 128)
            gate = post[own, at].astype(F32)
            made[own, at] = (wide[k, pl.ds(s, rows, stride=8), :] * gate).astype(BF16)
        copies.append(pltpu.make_async_copy(made.at[own], out.at[own], sems.at[k]))
        copies[-1].start()
    for copy in copies:
        copy.wait()


def body(pre_gate, value, post_gate, filter_taps, skip):
    tables = tuple(jnp.asarray(t) for t in build_tables())
    anyspace = pl.BlockSpec(memory_space=pl.ANY)
    vmem = pltpu.VMEM
    dma = pltpu.SemaphoreType.DMA
    whole = pl.BlockSpec(memory_space=vmem)
    conv, gate = pl.pallas_call(
        kernel,
        out_shape=[
            vmem((CTX * CH, 8, 128), BF16),
            vmem((CH, CHANNELS, PIECE), BF16),
        ],
        in_specs=[anyspace] * 10,
        out_specs=[whole, whole],
        scratch_shapes=[
            vmem((CHANNELS, BLOCK), BF16),
            vmem((CHANNELS, BLOCK), BF16),
            vmem((1, BLOCK), F32),
            vmem((2 * R, R), BF16),
            vmem((R, 2 * R), BF16),
            vmem((4 * R, R), BF16),
            vmem((4 * R, R), BF16),
            vmem((2, R, Q), F32),
            vmem((4, R, 128), F32),
            vmem((16, Q), F32),
            vmem((CTX, 16, Q), BF16),
            vmem((16, Q), BF16),
            vmem((CTX, 16, Q), BF16),
            vmem((CTX, 16, Q), BF16),
            vmem((8, 128), F32),
            vmem((8, 128), F32),
            vmem((4, R, 2 * 128), F32),
            vmem((4, R, 128), F32),
            vmem((CTX * CH * 8, 128), F32),
            vmem((CTX * CH, 8, 128), BF16),
            pltpu.SMEM((16,), F32),
            dma((4,)),
            dma((5,)),
            dma((2,)),
            dma((2,)),
            dma((2,)),
            dma((2,)),
            dma((2,)),
            dma((2,)),
        ],
        compiler_params=pltpu.CompilerParams(
            collective_id=0, has_side_effects=True, vmem_limit_bytes=56 * 1024 * 1024
        ),
        name="hyena",
    )(pre_gate, value, post_gate, filter_taps, skip, *tables)
    return pl.pallas_call(
        gate_kernel,
        out_shape=jax.ShapeDtypeStruct((CTX * CH, PIECE), BF16),
        in_specs=[whole, whole],
        out_specs=anyspace,
        scratch_shapes=[
            vmem((GATE_PARTS, CTX * CH * 8 // GATE_PARTS, 128), F32),
            vmem((CTX * CH, PIECE), BF16),
            dma((GATE_PARTS,)),
        ],
        compiler_params=pltpu.CompilerParams(vmem_limit_bytes=4 * 1024 * 1024),
        name="gate",
    )(conv, gate.reshape(CTX * CH, PIECE))


def solution(mesh):
    placed = (P("ch", "ctx"), P("ch", "ctx"), P("ch", "ctx"), P("ch", "ctx"), P("ch"))
    return jax.shard_map(
        body, mesh=mesh, in_specs=placed, out_specs=P(None, ("ctx", "ch")), check_vma=False
    )
```

```python
import jax
import jax.numpy as jnp
import numpy as np
import ml_dtypes
from jax import lax
from jax.experimental import pallas as pl
from jax.experimental.pallas import tpu as pltpu
from jax.sharding import PartitionSpec as P

MESH = pl.DeviceIdType.MESH
F32 = jnp.float32
BF16 = jnp.bfloat16

CTX_Y = 4
CTX = 16
CH = 8
HALF = 8
CHANNELS = 16
BLOCK = 8192
R = 256
Q = 512
GATE_PARTS = 4
PIECE = 1024


def ring(step):
    return min(step, 4 - step)


FAR_FIRST = sorted([(dx, dy) for dx in range(4) for dy in range(4)], key=lambda o: -(ring(o[0]) + ring(o[1])))


COLUMN = ((2, 0), (2, 1), (1, 0), (3, 0), (1, 1), (3, 1), (0, 1))


def pair(table, flip):
    re, im = table.real, table.imag
    return np.block([[re, im], [im, -re]]) if flip else np.block([[re, im], [-im, re]])


def build_tables():
    rows = np.arange(R)
    cols = np.arange(Q)
    part = np.arange(128)
    first = 2 * np.pi * ((np.outer(2 * rows + 1, rows)) % 1024) / 1024.0
    forward = np.concatenate([np.cos(first), -np.sin(first)], axis=0)
    order = np.concatenate([rows[0::2], rows[1::2]])
    backward = np.concatenate([np.cos(first).T, np.sin(first).T], axis=1)[order] * (2.0**-17)
    turn = 2 * np.pi * np.outer(2 * rows + 1, cols) / 2.0**19
    twiddle = np.stack([np.cos(turn), -np.sin(turn)])
    waves = [np.exp(-2j * np.pi * (np.outer(part, d + 4 * part) % Q) / Q) for d in range(4)]
    there = np.concatenate([pair(w, False) for w in waves], axis=0)
    back = np.concatenate([pair(w.T, True) for w in waves], axis=0)
    half = lambda a: a.astype(np.float32).astype(ml_dtypes.bfloat16)
    return half(forward), half(backward), half(there), half(back), twiddle.astype(np.float32)


def times(a, b):
    return a[0] * b[0] - a[1] * b[1], a[0] * b[1] + a[1] * b[0]


def four_point(v):
    (r0, i0), (r1, i1), (r2, i2), (r3, i3) = v
    sr, si, dr, di = r0 + r2, i0 + i2, r0 - r2, i0 - i2
    ur, ui, er, ei = r1 + r3, i1 + i3, r1 - r3, i1 - i3
    return [(sr + ur, si + ui), (dr + ei, di - er), (sr - ur, si - ui), (dr - ei, di + er)]


def kernel(
    pre, val, post, taps, skip_hbm, fwd_t, bwd_t, there_t, back_t, tw_t, y_out, post_out,
    pre_v, val_v, taps_v, fwd_v, bwd_v, there_v, back_v, tw_v,
    sig32, tap32, sig_send, tap_send, sig_recv, tap_recv, skip_send, skip_recv,
    spec_h, y32, lin32, y_send, y_first,
    skip, load_sems, table_sems, sig_sems, tap_sems, pass_sems, skip_sems, post_sems, y_sems, first_sem,
):
    p = lax.axis_index("ctx")
    g = lax.axis_index("ch")
    px, py = p // CTX_Y, p % CTX_Y
    z, core = g // 2, g % 2
    xs = [(px + i) % 4 for i in range(4)]
    ys = [(py + i) % 4 for i in range(4)]
    zs = [(z + i) % 4 for i in range(4)]
    cs = [core, 1 - core]
    sibling = z * 2 + 1 - core
    half = py // 2
    at_home = half == core
    own_group = z * 2 + half
    place = lax.rem(py, 2) * 4 + px
    own_channel = place * 2 + core
    taps_core = p // HALF

    near_y = 2 * core + lax.rem(py, 2)
    flip_y = 2 * core + 1 - lax.rem(py, 2)
    first_y = jnp.where(at_home, flip_y, near_y)
    last_y = jnp.where(at_home, near_y, flip_y)
    workers = [
        (xs[2], first_y), (xs[1], first_y), (xs[3], first_y), (xs[2], last_y),
        (xs[1], last_y), (xs[3], last_y), (xs[0], first_y), (xs[0], last_y),
    ]

    barrier = pltpu.get_barrier_semaphore()
    for dx in (2, 1, 3, 0):
        for dy in (2, 1, 3, 0):
            if dx or dy:
                pl.semaphore_signal(
                    barrier, inc=1, device_id=(xs[dx] * CTX_Y + ys[dy], z * 2 + half), device_id_type=MESH
                )
    for dz, dc in COLUMN:
        pl.semaphore_signal(barrier, inc=1, device_id=(p, zs[dz] * 2 + cs[dc]), device_id_type=MESH)

    loads = [
        pltpu.make_async_copy(a, b, load_sems.at[i])
        for i, (a, b) in enumerate([(taps, taps_v), (pre, pre_v), (val, val_v), (skip_hbm, skip)])
    ]
    tables = [
        pltpu.make_async_copy(a, b, table_sems.at[i])
        for i, (a, b) in enumerate([(fwd_t, fwd_v), (tw_t, tw_v), (there_t, there_v), (back_t, back_v), (bwd_t, bwd_v)])
    ]
    for c in loads + tables:
        c.start()

    loads[0].wait()
    for r in range(16):
        tap32[r : r + 1, :] = taps_v[0:1, r * Q : (r + 1) * Q]
    tap_send[...] = tap32[...].astype(BF16)
    loads[1].wait()
    loads[2].wait()
    for r in range(16):
        at = pl.ds(r * Q, Q)
        prod = pre_v[:, at].astype(F32) * val_v[:, at].astype(F32)
        for q in range(4):
            sig32[q, pl.ds(r, 16, stride=16), :] = prod[:, q * 128 : (q + 1) * 128]
    for q in range(4):
        sig_send[:, :, q * 128 : (q + 1) * 128] = (
            sig32[q].astype(BF16).reshape(CHANNELS, 16, 128)
        )

    @pl.when(at_home)
    def _():
        pl.semaphore_wait(barrier, 7 + 14)

    @pl.when(jnp.logical_not(at_home))
    def _():
        pl.semaphore_wait(barrier, 7 + 16)

    def send_taps(o):
        pltpu.make_async_remote_copy(
            tap_send, tap_recv.at[p], tap_sems.at[0], tap_sems.at[1],
            device_id=(o[0] * CTX_Y + o[1], z * 2 + taps_core), device_id_type=MESH,
        ).start()

    def send_signal(o, k):
        pltpu.make_async_remote_copy(
            sig_send.at[(lax.rem(o[1], 2) * 4 + o[0]) * 2 + k], sig_recv.at[p], sig_sems.at[0], sig_sems.at[1],
            device_id=(o[0] * CTX_Y + o[1], z * 2 + k), device_id_type=MESH,
        ).start()

    for o in workers[:-1]:
        send_taps(o)
    for o in workers[:-1]:
        send_signal(o, 0)
        send_signal(o, 1)
    keeps_taps = jnp.logical_and(at_home, taps_core == core)

    @pl.when(keeps_taps)
    def _():
        pltpu.make_async_copy(tap_send, tap_recv.at[p], tap_sems.at[1]).start()

    @pl.when(jnp.logical_not(keeps_taps))
    def _():
        send_taps(workers[-1])

    @pl.when(at_home)
    def _():
        pltpu.make_async_remote_copy(
            sig_send.at[place * 2 + 1 - core], sig_recv.at[p], sig_sems.at[0], sig_sems.at[1],
            device_id=(p, sibling), device_id_type=MESH,
        ).start()
        pltpu.make_async_copy(sig_send.at[own_channel], sig_recv.at[p], sig_sems.at[1]).start()

    @pl.when(jnp.logical_not(at_home))
    def _():
        send_signal(workers[-1], 0)
        send_signal(workers[-1], 1)

    loads[3].wait()
    skip_send[...] = jnp.full((8, 128), skip[place * 2 + 1 - core], F32)
    to_sibling = pltpu.make_async_remote_copy(
        skip_send, skip_recv, skip_sems.at[0], skip_sems.at[1],
        device_id=(p, sibling), device_id_type=MESH,
    )
    to_sibling.start()

    def post_part(o):
        return post.at[:, pl.ds(pl.multiple_of(o * PIECE, PIECE), PIECE)]

    for dz, dc in COLUMN:
        o = zs[dz] * 2 + cs[dc]
        pltpu.make_async_remote_copy(
            post_part(o), post_out.at[g], post_sems.at[0], post_sems.at[1],
            device_id=(p, o), device_id_type=MESH,
        ).start()
    pltpu.make_async_copy(post_part(g), post_out.at[g], post_sems.at[1]).start()

    def lanes(a):
        return slice(a * 128, (a + 1) * 128)

    def turn(a):
        return tw_v[0, :, lanes(a)], tw_v[1, :, lanes(a)]

    def joined(re, im):
        return jnp.concatenate([re.astype(BF16), im.astype(BF16)], axis=1)

    def spectrum(data):
        a = jnp.dot(fwd_v[...], data, preferred_element_type=F32)
        parts = four_point([times((a[:R, lanes(i)], a[R:, lanes(i)]), turn(i)) for i in range(4)])
        return [
            jnp.dot(joined(*parts[d]), there_v[d * R : (d + 1) * R, :], preferred_element_type=F32)
            for d in range(4)
        ]

    def pieces(signal):
        parts = []
        for d, part in enumerate(spectrum(signal)):
            prod = times((part[:, :128], part[:, 128:]), (spec_h[d, :, :128], spec_h[d, :, 128:]))
            part = jnp.dot(joined(*prod), back_v[d * R : (d + 1) * R, :], preferred_element_type=F32)
            parts.append((part[:, :128], part[:, 128:]))
        parts = [times(part, turn(i)) for i, part in enumerate(four_point(parts))]
        columns = jnp.concatenate(
            [jnp.concatenate([part[i].astype(BF16) for part in parts], axis=1) for i in range(2)], axis=0
        )
        conv = jnp.dot(bwd_v[...], columns, preferred_element_type=F32)
        for e in range(2):
            for q in range(4):
                lin32[pl.ds(e * 4 + q, 128, stride=8), :] = (
                    conv[e * 128 : (e + 1) * 128, lanes(q)] + y32[q, pl.ds(e, 128, stride=2), :]
                )
        return lin32[...].reshape(CTX * CH, 8, 128).astype(BF16)

    for c in tables:
        c.wait()

    @pl.when(p == 0)
    def _():
        gap = jnp.zeros((16, Q), BF16)
        first = jnp.concatenate([tap_send[...], jnp.zeros((R - 16, Q), BF16)], axis=0)
        for d, part in enumerate(spectrum(first)):
            spec_h[d] = part

        def eight_channels(r, carry):
            rows = []
            for i in range(8):
                own = sig_send[r * 8 + i]
                rows += [own, gap]
                for q in range(4):
                    y32[q, 32 * i : 32 * i + 16, :] = skip[r * 8 + i] * own[:, lanes(q)].astype(F32)
                    y32[q, 32 * i + 16 : 32 * i + 32, :] = jnp.zeros((16, 128), F32)
            y_first[r] = pieces(jnp.concatenate(rows, axis=0)).reshape(8, 16, 8, 128)
            to = pl.ds(g * CHANNELS + r * 8, 8)
            for dz, dc in COLUMN:
                o = zs[dz] * 2 + cs[dc]
                pltpu.make_async_remote_copy(
                    y_first.at[r, :, o], y_out.at[to], first_sem, y_sems.at[1],
                    device_id=(p, o), device_id_type=MESH,
                ).start()
            pltpu.make_async_copy(y_first.at[r, :, g], y_out.at[to], y_sems.at[1]).start()
            return carry

        lax.fori_loop(0, 2, eight_channels, 0)

    mine = tap_recv.at[pl.ds(core * HALF, HALF)]
    theirs = tap_recv.at[pl.ds((1 - core) * HALF, HALF)]
    pltpu.make_async_copy(mine, mine, tap_sems.at[1]).wait()
    passed = pltpu.make_async_remote_copy(
        mine, mine, pass_sems.at[0], pass_sems.at[1], device_id=(p, sibling), device_id_type=MESH
    )
    passed.start()

    pltpu.make_async_copy(theirs, theirs, pass_sems.at[1]).wait()
    for d, part in enumerate(spectrum(tap_recv[...].reshape(R, Q))):
        spec_h[d] = part

    pltpu.make_async_copy(sig_recv, sig_recv, sig_sems.at[1]).wait()
    signal = sig_recv[...].reshape(R, Q)
    to_sibling.wait_recv()
    weight = jnp.where(at_home, skip[own_channel], skip_recv[0:1, :])
    for q in range(4):
        y32[q] = weight * signal[:, lanes(q)].astype(F32)
    y_send[...] = pieces(signal)

    channel = own_group * CHANNELS + own_channel
    def send_piece(o_ctx, o_ch):
        pltpu.make_async_remote_copy(
            y_send.at[o_ctx * CH + o_ch], y_out.at[channel], y_sems.at[0], y_sems.at[1],
            device_id=(o_ctx, o_ch), device_id_type=MESH,
        ).start()

    for o_z in range(4):
        for dx, dy in FAR_FIRST:
            o_ctx = xs[dx] * CTX_Y + ys[dy]

            @pl.when(o_ctx != 0)
            def _(o_ctx=o_ctx, o_z=o_z, same=not (dx or dy)):
                for c in range(2):
                    if same:

                        @pl.when(g != o_z * 2 + c)
                        def _(c=c):
                            send_piece(o_ctx, o_z * 2 + c)

                    else:
                        send_piece(o_ctx, o_z * 2 + c)

    @pl.when(p != 0)
    def _():
        pltpu.make_async_copy(y_send.at[p * CH + g], y_out.at[channel], y_sems.at[1]).start()

    @pl.when(at_home)
    def _():
        part = sig_send.at[pl.ds(0, 15)]
        pltpu.make_async_copy(part, part, sig_sems.at[0]).wait()

    @pl.when(jnp.logical_not(at_home))
    def _():
        pltpu.make_async_copy(sig_send, sig_send, sig_sems.at[0]).wait()

    @pl.when(keeps_taps)
    def _():
        part = tap_recv.at[pl.ds(0, 7)]
        pltpu.make_async_copy(part, part, tap_sems.at[0]).wait()

    @pl.when(jnp.logical_not(keeps_taps))
    def _():
        part = tap_recv.at[pl.ds(0, 8)]
        pltpu.make_async_copy(part, part, tap_sems.at[0]).wait()

    passed.wait_send()
    to_sibling.wait_send()
    part = post_out.at[pl.ds(0, CH - 1)]
    pltpu.make_async_copy(part, part, post_sems.at[0]).wait()
    pltpu.make_async_copy(post_out, post_out, post_sems.at[1]).wait()

    @pl.when(p == 0)
    def _():
        part = y_send.at[pl.ds(0, (CTX - 1) * CH)]
        pltpu.make_async_copy(part, part, y_sems.at[0]).wait()
        part = y_send.at[pl.ds(0, 2 * 8 * (CH - 1))]
        pltpu.make_async_copy(part, part, first_sem).wait()

    @pl.when(p != 0)
    def _():
        part = y_send.at[pl.ds(0, (CTX - 1) * CH - 1)]
        pltpu.make_async_copy(part, part, y_sems.at[0]).wait()

    pltpu.make_async_copy(y_out, y_out, y_sems.at[1]).wait()


def gate_kernel(y, post, out, wide, made, sems):
    rows = CTX * CH // GATE_PARTS
    copies = []
    for k in range(GATE_PARTS):
        own = pl.ds(k * rows, rows)
        wide[k] = y[own].astype(F32).reshape(rows * 8, 128)
        for s in range(8):
            at = pl.ds(s * 128, 128)
            gate = post[own, at].astype(F32)
            made[own, at] = (wide[k, pl.ds(s, rows, stride=8), :] * gate).astype(BF16)
        copies.append(pltpu.make_async_copy(made.at[own], out.at[own], sems.at[k]))
        copies[-1].start()
    for copy in copies:
        copy.wait()


def body(pre_gate, value, post_gate, filter_taps, skip):
    tables = tuple(jnp.asarray(t) for t in build_tables())
    anyspace = pl.BlockSpec(memory_space=pl.ANY)
    vmem = pltpu.VMEM
    dma = pltpu.SemaphoreType.DMA
    whole = pl.BlockSpec(memory_space=vmem)
    conv, gate = pl.pallas_call(
        kernel,
        out_shape=[
            vmem((CTX * CH, 8, 128), BF16),
            vmem((CH, CHANNELS, PIECE), BF16),
        ],
        in_specs=[anyspace] * 10,
        out_specs=[whole, whole],
        scratch_shapes=[
            vmem((CHANNELS, BLOCK), BF16),
            vmem((CHANNELS, BLOCK), BF16),
            vmem((1, BLOCK), F32),
            vmem((2 * R, R), BF16),
            vmem((R, 2 * R), BF16),
            vmem((4 * R, R), BF16),
            vmem((4 * R, R), BF16),
            vmem((2, R, Q), F32),
            vmem((4, R, 128), F32),
            vmem((16, Q), F32),
            vmem((CTX, 16, Q), BF16),
            vmem((16, Q), BF16),
            vmem((CTX, 16, Q), BF16),
            vmem((CTX, 16, Q), BF16),
            vmem((8, 128), F32),
            vmem((8, 128), F32),
            vmem((4, R, 2 * 128), F32),
            vmem((4, R, 128), F32),
            vmem((CTX * CH * 8, 128), F32),
            vmem((CTX * CH, 8, 128), BF16),
            vmem((2, 8, 16, 8, 128), BF16),
            pltpu.SMEM((16,), F32),
            dma((4,)),
            dma((5,)),
            dma((2,)),
            dma((2,)),
            dma((2,)),
            dma((2,)),
            dma((2,)),
            dma((2,)),
            dma,
        ],
        compiler_params=pltpu.CompilerParams(
            collective_id=0, has_side_effects=True, vmem_limit_bytes=56 * 1024 * 1024
        ),
        name="hyena",
    )(pre_gate, value, post_gate, filter_taps, skip, *tables)
    return pl.pallas_call(
        gate_kernel,
        out_shape=jax.ShapeDtypeStruct((CTX * CH, PIECE), BF16),
        in_specs=[whole, whole],
        out_specs=anyspace,
        scratch_shapes=[
            vmem((GATE_PARTS, CTX * CH * 8 // GATE_PARTS, 128), F32),
            vmem((CTX * CH, PIECE), BF16),
            dma((GATE_PARTS,)),
        ],
        compiler_params=pltpu.CompilerParams(vmem_limit_bytes=4 * 1024 * 1024),
        name="gate",
    )(conv, gate.reshape(CTX * CH, PIECE))


def solution(mesh):
    placed = (P("ch", "ctx"), P("ch", "ctx"), P("ch", "ctx"), P("ch", "ctx"), P("ch"))
    return jax.shard_map(
        body, mesh=mesh, in_specs=placed, out_specs=P(None, ("ctx", "ch")), check_vma=False
    )
```

```python
import jax
import jax.numpy as jnp
import numpy as np
import ml_dtypes
from jax import lax
from jax.experimental import pallas as pl
from jax.experimental.pallas import tpu as pltpu
from jax.sharding import PartitionSpec as P

MESH = pl.DeviceIdType.MESH
F32 = jnp.float32
BF16 = jnp.bfloat16

CTX_Y = 4
CTX = 16
CH = 8
HALF = 8
CHANNELS = 16
BLOCK = 8192
R = 256
Q = 512
GATE_PARTS = 4
PIECE = 1024


def ring(step):
    return min(step, 4 - step)


FAR_FIRST = sorted([(dx, dy) for dx in range(4) for dy in range(4)], key=lambda o: -(ring(o[0]) + ring(o[1])))


COLUMN = ((2, 0), (2, 1), (1, 0), (3, 0), (1, 1), (3, 1), (0, 1))


def pair(table, flip):
    re, im = table.real, table.imag
    return np.block([[re, im], [im, -re]]) if flip else np.block([[re, im], [-im, re]])


def build_tables():
    rows = np.arange(R)
    cols = np.arange(Q)
    part = np.arange(128)
    first = 2 * np.pi * ((np.outer(2 * rows + 1, rows)) % 1024) / 1024.0
    forward = np.concatenate([np.cos(first), -np.sin(first)], axis=0)
    order = np.concatenate([rows[0::2], rows[1::2]])
    backward = np.concatenate([np.cos(first).T, np.sin(first).T], axis=1)[order] * (2.0**-17)
    turn = 2 * np.pi * np.outer(2 * rows + 1, cols) / 2.0**19
    twiddle = np.stack([np.cos(turn), -np.sin(turn)])
    waves = [np.exp(-2j * np.pi * (np.outer(part, d + 4 * part) % Q) / Q) for d in range(4)]
    there = np.concatenate([pair(w, False) for w in waves], axis=0)
    back = np.concatenate([pair(w.T, True) for w in waves], axis=0)
    half = lambda a: a.astype(np.float32).astype(ml_dtypes.bfloat16)
    return half(forward), half(backward), half(there), half(back), twiddle.astype(np.float32)


def times(a, b):
    return a[0] * b[0] - a[1] * b[1], a[0] * b[1] + a[1] * b[0]


def four_point(v):
    (r0, i0), (r1, i1), (r2, i2), (r3, i3) = v
    sr, si, dr, di = r0 + r2, i0 + i2, r0 - r2, i0 - i2
    ur, ui, er, ei = r1 + r3, i1 + i3, r1 - r3, i1 - i3
    return [(sr + ur, si + ui), (dr + ei, di - er), (sr - ur, si - ui), (dr - ei, di + er)]


def kernel(
    pre, val, post, taps, skip_hbm, fwd_t, bwd_t, there_t, back_t, tw_t, y_out, post_out,
    pre_v, val_v, taps_v, fwd_v, bwd_v, there_v, back_v, tw_v,
    sig32, tap32, sig_send, tap_send, sig_recv, tap_recv, skip_send, skip_recv,
    spec_h, y32, lin32, y_send, y_first,
    skip, load_sems, table_sems, sig_sems, tap_sems, pass_sems, skip_sems, post_sems, y_sems, first_sem,
):
    p = lax.axis_index("ctx")
    g = lax.axis_index("ch")
    px, py = p // CTX_Y, p % CTX_Y
    z, core = g // 2, g % 2
    xs = [(px + i) % 4 for i in range(4)]
    ys = [(py + i) % 4 for i in range(4)]
    zs = [(z + i) % 4 for i in range(4)]
    cs = [core, 1 - core]
    sibling = z * 2 + 1 - core
    half = py // 2
    at_home = half == core
    own_group = z * 2 + half
    place = lax.rem(py, 2) * 4 + px
    own_channel = place * 2 + core
    taps_core = p // HALF

    near_y = 2 * core + lax.rem(py, 2)
    flip_y = 2 * core + 1 - lax.rem(py, 2)
    first_y = jnp.where(at_home, flip_y, near_y)
    last_y = jnp.where(at_home, near_y, flip_y)
    workers = [
        (xs[2], first_y), (xs[1], first_y), (xs[3], first_y), (xs[2], last_y),
        (xs[1], last_y), (xs[3], last_y), (xs[0], first_y), (xs[0], last_y),
    ]

    barrier = pltpu.get_barrier_semaphore()
    for dx in (2, 1, 3, 0):
        for dy in (2, 1, 3, 0):
            if dx or dy:
                pl.semaphore_signal(
                    barrier, inc=1, device_id=(xs[dx] * CTX_Y + ys[dy], z * 2 + half), device_id_type=MESH
                )
    for dz, dc in COLUMN:
        pl.semaphore_signal(barrier, inc=1, device_id=(p, zs[dz] * 2 + cs[dc]), device_id_type=MESH)

    loads = [
        pltpu.make_async_copy(a, b, load_sems.at[i])
        for i, (a, b) in enumerate([(taps, taps_v), (pre, pre_v), (val, val_v), (skip_hbm, skip)])
    ]
    tables = [
        pltpu.make_async_copy(a, b, table_sems.at[i])
        for i, (a, b) in enumerate([(fwd_t, fwd_v), (tw_t, tw_v), (there_t, there_v), (back_t, back_v), (bwd_t, bwd_v)])
    ]
    for c in loads + tables:
        c.start()

    loads[0].wait()
    for r in range(16):
        tap32[r : r + 1, :] = taps_v[0:1, r * Q : (r + 1) * Q]
    tap_send[...] = tap32[...].astype(BF16)
    loads[1].wait()
    loads[2].wait()
    for r in range(16):
        at = pl.ds(r * Q, Q)
        prod = pre_v[:, at].astype(F32) * val_v[:, at].astype(F32)
        for q in range(4):
            sig32[q, pl.ds(r, 16, stride=16), :] = prod[:, q * 128 : (q + 1) * 128]
    for q in range(4):
        sig_send[:, :, q * 128 : (q + 1) * 128] = (
            sig32[q].astype(BF16).reshape(CHANNELS, 16, 128)
        )

    @pl.when(at_home)
    def _():
        pl.semaphore_wait(barrier, 7 + 14)

    @pl.when(jnp.logical_not(at_home))
    def _():
        pl.semaphore_wait(barrier, 7 + 16)

    def send_taps(o):
        pltpu.make_async_remote_copy(
            tap_send, tap_recv.at[p], tap_sems.at[0], tap_sems.at[1],
            device_id=(o[0] * CTX_Y + o[1], z * 2 + taps_core), device_id_type=MESH,
        ).start()

    def send_signal(o, k):
        pltpu.make_async_remote_copy(
            sig_send.at[(lax.rem(o[1], 2) * 4 + o[0]) * 2 + k], sig_recv.at[p], sig_sems.at[0], sig_sems.at[1],
            device_id=(o[0] * CTX_Y + o[1], z * 2 + k), device_id_type=MESH,
        ).start()

    for o in workers[:-1]:
        send_taps(o)
    for k in range(2):
        for o in workers[:-1]:
            send_signal(o, k)
    keeps_taps = jnp.logical_and(at_home, taps_core == core)

    @pl.when(keeps_taps)
    def _():
        pltpu.make_async_copy(tap_send, tap_recv.at[p], tap_sems.at[1]).start()

    @pl.when(jnp.logical_not(keeps_taps))
    def _():
        send_taps(workers[-1])

    @pl.when(at_home)
    def _():
        pltpu.make_async_remote_copy(
            sig_send.at[place * 2 + 1 - core], sig_recv.at[p], sig_sems.at[0], sig_sems.at[1],
            device_id=(p, sibling), device_id_type=MESH,
        ).start()
        pltpu.make_async_copy(sig_send.at[own_channel], sig_recv.at[p], sig_sems.at[1]).start()

    @pl.when(jnp.logical_not(at_home))
    def _():
        send_signal(workers[-1], 0)
        send_signal(workers[-1], 1)

    loads[3].wait()
    skip_send[...] = jnp.full((8, 128), skip[place * 2 + 1 - core], F32)
    to_sibling = pltpu.make_async_remote_copy(
        skip_send, skip_recv, skip_sems.at[0], skip_sems.at[1],
        device_id=(p, sibling), device_id_type=MESH,
    )
    to_sibling.start()

    def post_part(o):
        return post.at[:, pl.ds(pl.multiple_of(o * PIECE, PIECE), PIECE)]

    for dz, dc in COLUMN:
        o = zs[dz] * 2 + cs[dc]
        pltpu.make_async_remote_copy(
            post_part(o), post_out.at[g], post_sems.at[0], post_sems.at[1],
            device_id=(p, o), device_id_type=MESH,
        ).start()
    pltpu.make_async_copy(post_part(g), post_out.at[g], post_sems.at[1]).start()

    def lanes(a):
        return slice(a * 128, (a + 1) * 128)

    def turn(a):
        return tw_v[0, :, lanes(a)], tw_v[1, :, lanes(a)]

    def joined(re, im):
        return jnp.concatenate([re.astype(BF16), im.astype(BF16)], axis=1)

    def spectrum(data):
        a = jnp.dot(fwd_v[...], data, preferred_element_type=F32)
        parts = four_point([times((a[:R, lanes(i)], a[R:, lanes(i)]), turn(i)) for i in range(4)])
        return [
            jnp.dot(joined(*parts[d]), there_v[d * R : (d + 1) * R, :], preferred_element_type=F32)
            for d in range(4)
        ]

    def pieces(signal):
        parts = []
        for d, part in enumerate(spectrum(signal)):
            prod = times((part[:, :128], part[:, 128:]), (spec_h[d, :, :128], spec_h[d, :, 128:]))
            part = jnp.dot(joined(*prod), back_v[d * R : (d + 1) * R, :], preferred_element_type=F32)
            parts.append((part[:, :128], part[:, 128:]))
        parts = [times(part, turn(i)) for i, part in enumerate(four_point(parts))]
        columns = jnp.concatenate(
            [jnp.concatenate([part[i].astype(BF16) for part in parts], axis=1) for i in range(2)], axis=0
        )
        conv = jnp.dot(bwd_v[...], columns, preferred_element_type=F32)
        for e in range(2):
            for q in range(4):
                lin32[pl.ds(e * 4 + q, 128, stride=8), :] = (
                    conv[e * 128 : (e + 1) * 128, lanes(q)] + y32[q, pl.ds(e, 128, stride=2), :]
                )
        return lin32[...].reshape(CTX * CH, 8, 128).astype(BF16)

    for c in tables:
        c.wait()

    @pl.when(p == 0)
    def _():
        gap = jnp.zeros((16, Q), BF16)
        first = jnp.concatenate([tap_send[...], jnp.zeros((R - 16, Q), BF16)], axis=0)
        for d, part in enumerate(spectrum(first)):
            spec_h[d] = part

        def eight_channels(r, carry):
            rows = []
            for i in range(8):
                own = sig_send[r * 8 + i]
                rows += [own, gap]
                for q in range(4):
                    y32[q, 32 * i : 32 * i + 16, :] = skip[r * 8 + i] * own[:, lanes(q)].astype(F32)
                    y32[q, 32 * i + 16 : 32 * i + 32, :] = jnp.zeros((16, 128), F32)
            y_first[r] = pieces(jnp.concatenate(rows, axis=0)).reshape(8, 16, 8, 128)
            to = pl.ds(g * CHANNELS + r * 8, 8)
            for dz, dc in COLUMN:
                o = zs[dz] * 2 + cs[dc]
                pltpu.make_async_remote_copy(
                    y_first.at[r, :, o], y_out.at[to], first_sem, y_sems.at[1],
                    device_id=(p, o), device_id_type=MESH,
                ).start()
            pltpu.make_async_copy(y_first.at[r, :, g], y_out.at[to], y_sems.at[1]).start()
            return carry

        lax.fori_loop(0, 2, eight_channels, 0)

    mine = tap_recv.at[pl.ds(core * HALF, HALF)]
    theirs = tap_recv.at[pl.ds((1 - core) * HALF, HALF)]
    pltpu.make_async_copy(mine, mine, tap_sems.at[1]).wait()
    passed = pltpu.make_async_remote_copy(
        mine, mine, pass_sems.at[0], pass_sems.at[1], device_id=(p, sibling), device_id_type=MESH
    )
    passed.start()

    pltpu.make_async_copy(theirs, theirs, pass_sems.at[1]).wait()
    for d, part in enumerate(spectrum(tap_recv[...].reshape(R, Q))):
        spec_h[d] = part

    pltpu.make_async_copy(sig_recv, sig_recv, sig_sems.at[1]).wait()
    signal = sig_recv[...].reshape(R, Q)
    to_sibling.wait_recv()
    weight = jnp.where(at_home, skip[own_channel], skip_recv[0:1, :])
    for q in range(4):
        y32[q] = weight * signal[:, lanes(q)].astype(F32)
    y_send[...] = pieces(signal)

    channel = own_group * CHANNELS + own_channel
    def send_piece(o_ctx, o_ch):
        pltpu.make_async_remote_copy(
            y_send.at[o_ctx * CH + o_ch], y_out.at[channel], y_sems.at[0], y_sems.at[1],
            device_id=(o_ctx, o_ch), device_id_type=MESH,
        ).start()

    for o_z in range(4):
        for dx, dy in FAR_FIRST:
            o_ctx = xs[dx] * CTX_Y + ys[dy]

            @pl.when(o_ctx != 0)
            def _(o_ctx=o_ctx, o_z=o_z, same=not (dx or dy)):
                for c in range(2):
                    if same:

                        @pl.when(g != o_z * 2 + c)
                        def _(c=c):
                            send_piece(o_ctx, o_z * 2 + c)

                    else:
                        send_piece(o_ctx, o_z * 2 + c)

    @pl.when(p != 0)
    def _():
        pltpu.make_async_copy(y_send.at[p * CH + g], y_out.at[channel], y_sems.at[1]).start()

    @pl.when(at_home)
    def _():
        part = sig_send.at[pl.ds(0, 15)]
        pltpu.make_async_copy(part, part, sig_sems.at[0]).wait()

    @pl.when(jnp.logical_not(at_home))
    def _():
        pltpu.make_async_copy(sig_send, sig_send, sig_sems.at[0]).wait()

    @pl.when(keeps_taps)
    def _():
        part = tap_recv.at[pl.ds(0, 7)]
        pltpu.make_async_copy(part, part, tap_sems.at[0]).wait()

    @pl.when(jnp.logical_not(keeps_taps))
    def _():
        part = tap_recv.at[pl.ds(0, 8)]
        pltpu.make_async_copy(part, part, tap_sems.at[0]).wait()

    passed.wait_send()
    to_sibling.wait_send()
    part = post_out.at[pl.ds(0, CH - 1)]
    pltpu.make_async_copy(part, part, post_sems.at[0]).wait()
    pltpu.make_async_copy(post_out, post_out, post_sems.at[1]).wait()

    @pl.when(p == 0)
    def _():
        part = y_send.at[pl.ds(0, (CTX - 1) * CH)]
        pltpu.make_async_copy(part, part, y_sems.at[0]).wait()
        part = y_send.at[pl.ds(0, 2 * 8 * (CH - 1))]
        pltpu.make_async_copy(part, part, first_sem).wait()

    @pl.when(p != 0)
    def _():
        part = y_send.at[pl.ds(0, (CTX - 1) * CH - 1)]
        pltpu.make_async_copy(part, part, y_sems.at[0]).wait()

    pltpu.make_async_copy(y_out, y_out, y_sems.at[1]).wait()


def gate_kernel(y, post, out, wide, made, sems):
    rows = CTX * CH // GATE_PARTS
    copies = []
    for k in range(GATE_PARTS):
        own = pl.ds(k * rows, rows)
        wide[k] = y[own].astype(F32).reshape(rows * 8, 128)
        for s in range(8):
            at = pl.ds(s * 128, 128)
            gate = post[own, at].astype(F32)
            made[own, at] = (wide[k, pl.ds(s, rows, stride=8), :] * gate).astype(BF16)
        copies.append(pltpu.make_async_copy(made.at[own], out.at[own], sems.at[k]))
        copies[-1].start()
    for copy in copies:
        copy.wait()


def body(pre_gate, value, post_gate, filter_taps, skip):
    tables = tuple(jnp.asarray(t) for t in build_tables())
    anyspace = pl.BlockSpec(memory_space=pl.ANY)
    vmem = pltpu.VMEM
    dma = pltpu.SemaphoreType.DMA
    whole = pl.BlockSpec(memory_space=vmem)
    conv, gate = pl.pallas_call(
        kernel,
        out_shape=[
            vmem((CTX * CH, 8, 128), BF16),
            vmem((CH, CHANNELS, PIECE), BF16),
        ],
        in_specs=[anyspace] * 10,
        out_specs=[whole, whole],
        scratch_shapes=[
            vmem((CHANNELS, BLOCK), BF16),
            vmem((CHANNELS, BLOCK), BF16),
            vmem((1, BLOCK), F32),
            vmem((2 * R, R), BF16),
            vmem((R, 2 * R), BF16),
            vmem((4 * R, R), BF16),
            vmem((4 * R, R), BF16),
            vmem((2, R, Q), F32),
            vmem((4, R, 128), F32),
            vmem((16, Q), F32),
            vmem((CTX, 16, Q), BF16),
            vmem((16, Q), BF16),
            vmem((CTX, 16, Q), BF16),
            vmem((CTX, 16, Q), BF16),
            vmem((8, 128), F32),
            vmem((8, 128), F32),
            vmem((4, R, 2 * 128), F32),
            vmem((4, R, 128), F32),
            vmem((CTX * CH * 8, 128), F32),
            vmem((CTX * CH, 8, 128), BF16),
            vmem((2, 8, 16, 8, 128), BF16),
            pltpu.SMEM((16,), F32),
            dma((4,)),
            dma((5,)),
            dma((2,)),
            dma((2,)),
            dma((2,)),
            dma((2,)),
            dma((2,)),
            dma((2,)),
            dma,
        ],
        compiler_params=pltpu.CompilerParams(
            collective_id=0, has_side_effects=True, vmem_limit_bytes=56 * 1024 * 1024
        ),
        name="hyena",
    )(pre_gate, value, post_gate, filter_taps, skip, *tables)
    return pl.pallas_call(
        gate_kernel,
        out_shape=jax.ShapeDtypeStruct((CTX * CH, PIECE), BF16),
        in_specs=[whole, whole],
        out_specs=anyspace,
        scratch_shapes=[
            vmem((GATE_PARTS, CTX * CH * 8 // GATE_PARTS, 128), F32),
            vmem((CTX * CH, PIECE), BF16),
            dma((GATE_PARTS,)),
        ],
        compiler_params=pltpu.CompilerParams(vmem_limit_bytes=4 * 1024 * 1024),
        name="gate",
    )(conv, gate.reshape(CTX * CH, PIECE))


def solution(mesh):
    placed = (P("ch", "ctx"), P("ch", "ctx"), P("ch", "ctx"), P("ch", "ctx"), P("ch"))
    return jax.shard_map(
        body, mesh=mesh, in_specs=placed, out_specs=P(None, ("ctx", "ch")), check_vma=False
    )
```

```python
import jax
import jax.numpy as jnp
import numpy as np
import ml_dtypes
from jax import lax
from jax.experimental import pallas as pl
from jax.experimental.pallas import tpu as pltpu
from jax.sharding import PartitionSpec as P

MESH = pl.DeviceIdType.MESH
F32 = jnp.float32
BF16 = jnp.bfloat16

CTX_Y = 4
CTX = 16
CH = 8
HALF = 8
CHANNELS = 16
BLOCK = 8192
R = 256
Q = 512
GATE_PARTS = 4
PIECE = 1024


def ring(step):
    return min(step, 4 - step)


FAR_FIRST = sorted([(dx, dy) for dx in range(4) for dy in range(4)], key=lambda o: -(ring(o[0]) + ring(o[1])))


COLUMN = ((2, 0), (2, 1), (1, 0), (3, 0), (1, 1), (3, 1), (0, 1))


def pair(table, flip):
    re, im = table.real, table.imag
    return np.block([[re, im], [im, -re]]) if flip else np.block([[re, im], [-im, re]])


def build_tables():
    rows = np.arange(R)
    cols = np.arange(Q)
    part = np.arange(128)
    first = 2 * np.pi * ((np.outer(2 * rows + 1, rows)) % 1024) / 1024.0
    forward = np.concatenate([np.cos(first), -np.sin(first)], axis=0)
    pairs = rows.reshape(CTX, 2, 4, 2)
    order = pairs.transpose(1, 3, 0, 2).reshape(-1)
    backward = np.concatenate([np.cos(first).T, np.sin(first).T], axis=1)[order] * (2.0**-17)
    turn = 2 * np.pi * np.outer(2 * rows + 1, cols) / 2.0**19
    twiddle = np.stack([np.cos(turn), -np.sin(turn)])
    waves = [np.exp(-2j * np.pi * (np.outer(part, d + 4 * part) % Q) / Q) for d in range(4)]
    there = np.concatenate([pair(w, False) for w in waves], axis=0)
    back = np.concatenate([pair(w.T, True) for w in waves], axis=0)
    half = lambda a: a.astype(np.float32).astype(ml_dtypes.bfloat16)
    return half(forward), half(backward), half(there), half(back), twiddle.astype(np.float32)


def times(a, b):
    return a[0] * b[0] - a[1] * b[1], a[0] * b[1] + a[1] * b[0]


def four_point(v):
    (r0, i0), (r1, i1), (r2, i2), (r3, i3) = v
    sr, si, dr, di = r0 + r2, i0 + i2, r0 - r2, i0 - i2
    ur, ui, er, ei = r1 + r3, i1 + i3, r1 - r3, i1 - i3
    return [(sr + ur, si + ui), (dr + ei, di - er), (sr - ur, si - ui), (dr - ei, di + er)]


def kernel(
    pre, val, post, taps, skip_hbm, fwd_t, bwd_t, there_t, back_t, tw_t, y_out, post_out,
    pre_v, val_v, taps_v, fwd_v, bwd_v, there_v, back_v, tw_v,
    sig32, tap32, sig_send, tap_send, sig_recv, tap_recv, skip_send, skip_recv,
    spec_h, y32, direct, lin32, y_send, y_first,
    skip, load_sems, table_sems, sig_sems, tap_sems, pass_sems, skip_sems, post_sems, y_sems, first_sem,
):
    p = lax.axis_index("ctx")
    g = lax.axis_index("ch")
    px, py = p // CTX_Y, p % CTX_Y
    z, core = g // 2, g % 2
    xs = [(px + i) % 4 for i in range(4)]
    ys = [(py + i) % 4 for i in range(4)]
    zs = [(z + i) % 4 for i in range(4)]
    cs = [core, 1 - core]
    sibling = z * 2 + 1 - core
    half = py // 2
    at_home = half == core
    own_group = z * 2 + half
    place = lax.rem(py, 2) * 4 + px
    own_channel = place * 2 + core
    taps_core = p // HALF

    near_y = 2 * core + lax.rem(py, 2)
    flip_y = 2 * core + 1 - lax.rem(py, 2)
    first_y = jnp.where(at_home, flip_y, near_y)
    last_y = jnp.where(at_home, near_y, flip_y)
    workers = [
        (xs[2], first_y), (xs[1], first_y), (xs[3], first_y), (xs[2], last_y),
        (xs[1], last_y), (xs[3], last_y), (xs[0], first_y), (xs[0], last_y),
    ]

    barrier = pltpu.get_barrier_semaphore()
    for dx in (2, 1, 3, 0):
        for dy in (2, 1, 3, 0):
            if dx or dy:
                pl.semaphore_signal(
                    barrier, inc=1, device_id=(xs[dx] * CTX_Y + ys[dy], z * 2 + half), device_id_type=MESH
                )
    for dz, dc in COLUMN:
        pl.semaphore_signal(barrier, inc=1, device_id=(p, zs[dz] * 2 + cs[dc]), device_id_type=MESH)

    loads = [
        pltpu.make_async_copy(a, b, load_sems.at[i])
        for i, (a, b) in enumerate([(taps, taps_v), (pre, pre_v), (val, val_v), (skip_hbm, skip)])
    ]
    tables = [
        pltpu.make_async_copy(a, b, table_sems.at[i])
        for i, (a, b) in enumerate([(fwd_t, fwd_v), (tw_t, tw_v), (there_t, there_v), (back_t, back_v), (bwd_t, bwd_v)])
    ]
    for c in loads + tables:
        c.start()

    loads[0].wait()
    for r in range(16):
        tap32[r : r + 1, :] = taps_v[0:1, r * Q : (r + 1) * Q]
    tap_send[...] = tap32[...].astype(BF16)
    loads[1].wait()
    loads[2].wait()
    for r in range(16):
        at = pl.ds(r * Q, Q)
        prod = pre_v[:, at].astype(F32) * val_v[:, at].astype(F32)
        for q in range(4):
            sig32[q, pl.ds(r, 16, stride=16), :] = prod[:, q * 128 : (q + 1) * 128]
    for q in range(4):
        sig_send[:, :, q * 128 : (q + 1) * 128] = (
            sig32[q].astype(BF16).reshape(CHANNELS, 16, 128)
        )

    @pl.when(at_home)
    def _():
        pl.semaphore_wait(barrier, 7 + 14)

    @pl.when(jnp.logical_not(at_home))
    def _():
        pl.semaphore_wait(barrier, 7 + 16)

    def send_taps(o):
        pltpu.make_async_remote_copy(
            tap_send, tap_recv.at[p], tap_sems.at[0], tap_sems.at[1],
            device_id=(o[0] * CTX_Y + o[1], z * 2 + taps_core), device_id_type=MESH,
        ).start()

    def send_signal(o, k):
        pltpu.make_async_remote_copy(
            sig_send.at[(lax.rem(o[1], 2) * 4 + o[0]) * 2 + k], sig_recv.at[p], sig_sems.at[0], sig_sems.at[1],
            device_id=(o[0] * CTX_Y + o[1], z * 2 + k), device_id_type=MESH,
        ).start()

    for o in workers[:-1]:
        send_taps(o)
    for k in range(2):
        for o in workers[:-1]:
            send_signal(o, k)
    keeps_taps = jnp.logical_and(at_home, taps_core == core)

    @pl.when(keeps_taps)
    def _():
        pltpu.make_async_copy(tap_send, tap_recv.at[p], tap_sems.at[1]).start()

    @pl.when(jnp.logical_not(keeps_taps))
    def _():
        send_taps(workers[-1])

    @pl.when(at_home)
    def _():
        pltpu.make_async_remote_copy(
            sig_send.at[place * 2 + 1 - core], sig_recv.at[p], sig_sems.at[0], sig_sems.at[1],
            device_id=(p, sibling), device_id_type=MESH,
        ).start()
        pltpu.make_async_copy(sig_send.at[own_channel], sig_recv.at[p], sig_sems.at[1]).start()

    @pl.when(jnp.logical_not(at_home))
    def _():
        send_signal(workers[-1], 0)
        send_signal(workers[-1], 1)

    loads[3].wait()
    skip_send[...] = jnp.full((8, 128), skip[place * 2 + 1 - core], F32)
    to_sibling = pltpu.make_async_remote_copy(
        skip_send, skip_recv, skip_sems.at[0], skip_sems.at[1],
        device_id=(p, sibling), device_id_type=MESH,
    )
    to_sibling.start()

    def post_part(o):
        return post.at[:, pl.ds(pl.multiple_of(o * PIECE, PIECE), PIECE)]

    for dz, dc in COLUMN:
        o = zs[dz] * 2 + cs[dc]
        pltpu.make_async_remote_copy(
            post_part(o), post_out.at[g], post_sems.at[0], post_sems.at[1],
            device_id=(p, o), device_id_type=MESH,
        ).start()
    pltpu.make_async_copy(post_part(g), post_out.at[g], post_sems.at[1]).start()

    def lanes(a):
        return slice(a * 128, (a + 1) * 128)

    def turn(a):
        return tw_v[0, :, lanes(a)], tw_v[1, :, lanes(a)]

    def joined(re, im):
        return jnp.concatenate([re.astype(BF16), im.astype(BF16)], axis=1)

    def spectrum(data):
        a = jnp.dot(fwd_v[...], data, preferred_element_type=F32)
        parts = four_point([times((a[:R, lanes(i)], a[R:, lanes(i)]), turn(i)) for i in range(4)])
        return [
            jnp.dot(joined(*parts[d]), there_v[d * R : (d + 1) * R, :], preferred_element_type=F32)
            for d in range(4)
        ]

    def answer(signal):
        for e in range(2):
            for q in range(4):
                direct[pl.ds(e * 4 + q, 128, stride=8), :] = y32[q, pl.ds(e, 128, stride=2), :]
        parts = []
        for d, part in enumerate(spectrum(signal)):
            prod = times((part[:, :128], part[:, 128:]), (spec_h[d, :, :128], spec_h[d, :, 128:]))
            part = jnp.dot(joined(*prod), back_v[d * R : (d + 1) * R, :], preferred_element_type=F32)
            parts.append((part[:, :128], part[:, 128:]))
        parts = [times(part, turn(i)) for i, part in enumerate(four_point(parts))]
        return jnp.concatenate(
            [jnp.concatenate([part[i].astype(BF16) for part in parts], axis=1) for i in range(2)], axis=0
        )

    def pieces(columns, h):
        conv = jnp.dot(bwd_v[h * 128 : (h + 1) * 128], columns, preferred_element_type=F32)
        for e in range(2):
            for q in range(4):
                lin32[h, pl.ds(e * 4 + q, 64, stride=8), :] = conv[e * 64 : (e + 1) * 64, lanes(q)]
        total = lin32[h].reshape(CTX, 32, 128) + direct[...].reshape(CTX, 2, 32, 128)[:, h]
        return total.reshape(CTX, 4, 8, 128).astype(BF16)

    for c in tables:
        c.wait()

    @pl.when(p == 0)
    def _():
        gap = jnp.zeros((16, Q), BF16)
        first = jnp.concatenate([tap_send[...], jnp.zeros((R - 16, Q), BF16)], axis=0)
        for d, part in enumerate(spectrum(first)):
            spec_h[d] = part

        def eight_channels(r, carry):
            rows = []
            for i in range(8):
                own = sig_send[r * 8 + i]
                rows += [own, gap]
                for q in range(4):
                    y32[q, 32 * i : 32 * i + 16, :] = skip[r * 8 + i] * own[:, lanes(q)].astype(F32)
                    y32[q, 32 * i + 16 : 32 * i + 32, :] = jnp.zeros((16, 128), F32)
            columns = answer(jnp.concatenate(rows, axis=0))
            for h in range(2):
                part = pieces(columns, h).reshape(8, 2, 4, 8, 128)
                for k in range(2):
                    y_first[r, :, k * 8 + 4 * h : k * 8 + 4 * h + 4] = part[:, k]
            to = pl.ds(g * CHANNELS + r * 8, 8)
            for dz, dc in COLUMN:
                o = zs[dz] * 2 + cs[dc]
                pltpu.make_async_remote_copy(
                    y_first.at[r, :, o], y_out.at[to], first_sem, y_sems.at[1],
                    device_id=(p, o), device_id_type=MESH,
                ).start()
            pltpu.make_async_copy(y_first.at[r, :, g], y_out.at[to], y_sems.at[1]).start()
            return carry

        lax.fori_loop(0, 2, eight_channels, 0)

    mine = tap_recv.at[pl.ds(core * HALF, HALF)]
    theirs = tap_recv.at[pl.ds((1 - core) * HALF, HALF)]
    pltpu.make_async_copy(mine, mine, tap_sems.at[1]).wait()
    passed = pltpu.make_async_remote_copy(
        mine, mine, pass_sems.at[0], pass_sems.at[1], device_id=(p, sibling), device_id_type=MESH
    )
    passed.start()

    pltpu.make_async_copy(theirs, theirs, pass_sems.at[1]).wait()
    for d, part in enumerate(spectrum(tap_recv[...].reshape(R, Q))):
        spec_h[d] = part

    pltpu.make_async_copy(sig_recv, sig_recv, sig_sems.at[1]).wait()
    signal = sig_recv[...].reshape(R, Q)
    to_sibling.wait_recv()
    weight = jnp.where(at_home, skip[own_channel], skip_recv[0:1, :])
    for q in range(4):
        y32[q] = weight * signal[:, lanes(q)].astype(F32)
    columns = answer(signal)

    channel = own_group * CHANNELS + own_channel
    def send_piece(o_ctx, o_ch):
        pltpu.make_async_remote_copy(
            y_send.at[o_ctx, o_ch], y_out.at[channel], y_sems.at[0], y_sems.at[1],
            device_id=(o_ctx, o_ch), device_id_type=MESH,
        ).start()

    for o_z in range(4):
        if o_z % 2 == 0:
            y_send[:, o_z * 2 : o_z * 2 + 4] = pieces(columns, o_z // 2)
        for dx, dy in FAR_FIRST:
            o_ctx = xs[dx] * CTX_Y + ys[dy]

            @pl.when(o_ctx != 0)
            def _(o_ctx=o_ctx, o_z=o_z, same=not (dx or dy)):
                for c in range(2):
                    if same:

                        @pl.when(g != o_z * 2 + c)
                        def _(c=c):
                            send_piece(o_ctx, o_z * 2 + c)

                    else:
                        send_piece(o_ctx, o_z * 2 + c)

    @pl.when(p != 0)
    def _():
        pltpu.make_async_copy(y_send.at[p, g], y_out.at[channel], y_sems.at[1]).start()

    @pl.when(at_home)
    def _():
        part = sig_send.at[pl.ds(0, 15)]
        pltpu.make_async_copy(part, part, sig_sems.at[0]).wait()

    @pl.when(jnp.logical_not(at_home))
    def _():
        pltpu.make_async_copy(sig_send, sig_send, sig_sems.at[0]).wait()

    @pl.when(keeps_taps)
    def _():
        part = tap_recv.at[pl.ds(0, 7)]
        pltpu.make_async_copy(part, part, tap_sems.at[0]).wait()

    @pl.when(jnp.logical_not(keeps_taps))
    def _():
        part = tap_recv.at[pl.ds(0, 8)]
        pltpu.make_async_copy(part, part, tap_sems.at[0]).wait()

    passed.wait_send()
    to_sibling.wait_send()
    part = post_out.at[pl.ds(0, CH - 1)]
    pltpu.make_async_copy(part, part, post_sems.at[0]).wait()
    pltpu.make_async_copy(post_out, post_out, post_sems.at[1]).wait()

    @pl.when(p == 0)
    def _():
        part = y_out.at[pl.ds(0, (CTX - 1) * CH)]
        pltpu.make_async_copy(part, part, y_sems.at[0]).wait()
        part = y_out.at[pl.ds(0, 2 * 8 * (CH - 1))]
        pltpu.make_async_copy(part, part, first_sem).wait()

    @pl.when(p != 0)
    def _():
        part = y_out.at[pl.ds(0, (CTX - 1) * CH - 1)]
        pltpu.make_async_copy(part, part, y_sems.at[0]).wait()

    pltpu.make_async_copy(y_out, y_out, y_sems.at[1]).wait()


def gate_kernel(y, post, out, wide, made, sems):
    rows = CTX * CH // GATE_PARTS
    copies = []
    for k in range(GATE_PARTS):
        own = pl.ds(k * rows, rows)
        wide[k] = y[own].astype(F32).reshape(rows * 8, 128)
        for s in range(8):
            at = pl.ds(s * 128, 128)
            gate = post[own, at].astype(F32)
            made[own, at] = (wide[k, pl.ds(s, rows, stride=8), :] * gate).astype(BF16)
        copies.append(pltpu.make_async_copy(made.at[own], out.at[own], sems.at[k]))
        copies[-1].start()
    for copy in copies:
        copy.wait()


def body(pre_gate, value, post_gate, filter_taps, skip):
    tables = tuple(jnp.asarray(t) for t in build_tables())
    anyspace = pl.BlockSpec(memory_space=pl.ANY)
    vmem = pltpu.VMEM
    dma = pltpu.SemaphoreType.DMA
    whole = pl.BlockSpec(memory_space=vmem)
    conv, gate = pl.pallas_call(
        kernel,
        out_shape=[
            vmem((CTX * CH, 8, 128), BF16),
            vmem((CH, CHANNELS, PIECE), BF16),
        ],
        in_specs=[anyspace] * 10,
        out_specs=[whole, whole],
        scratch_shapes=[
            vmem((CHANNELS, BLOCK), BF16),
            vmem((CHANNELS, BLOCK), BF16),
            vmem((1, BLOCK), F32),
            vmem((2 * R, R), BF16),
            vmem((R, 2 * R), BF16),
            vmem((4 * R, R), BF16),
            vmem((4 * R, R), BF16),
            vmem((2, R, Q), F32),
            vmem((4, R, 128), F32),
            vmem((16, Q), F32),
            vmem((CTX, 16, Q), BF16),
            vmem((16, Q), BF16),
            vmem((CTX, 16, Q), BF16),
            vmem((CTX, 16, Q), BF16),
            vmem((8, 128), F32),
            vmem((8, 128), F32),
            vmem((4, R, 2 * 128), F32),
            vmem((4, R, 128), F32),
            vmem((CTX * CH * 8, 128), F32),
            vmem((2, CTX * CH * 4, 128), F32),
            vmem((CTX, CH, 8, 128), BF16),
            vmem((2, 8, 16, 8, 128), BF16),
            pltpu.SMEM((16,), F32),
            dma((4,)),
            dma((5,)),
            dma((2,)),
            dma((2,)),
            dma((2,)),
            dma((2,)),
            dma((2,)),
            dma((2,)),
            dma,
        ],
        compiler_params=pltpu.CompilerParams(
            collective_id=0, has_side_effects=True, vmem_limit_bytes=56 * 1024 * 1024
        ),
        name="hyena",
    )(pre_gate, value, post_gate, filter_taps, skip, *tables)
    return pl.pallas_call(
        gate_kernel,
        out_shape=jax.ShapeDtypeStruct((CTX * CH, PIECE), BF16),
        in_specs=[whole, whole],
        out_specs=anyspace,
        scratch_shapes=[
            vmem((GATE_PARTS, CTX * CH * 8 // GATE_PARTS, 128), F32),
            vmem((CTX * CH, PIECE), BF16),
            dma((GATE_PARTS,)),
        ],
        compiler_params=pltpu.CompilerParams(vmem_limit_bytes=4 * 1024 * 1024),
        name="gate",
    )(conv, gate.reshape(CTX * CH, PIECE))


def solution(mesh):
    placed = (P("ch", "ctx"), P("ch", "ctx"), P("ch", "ctx"), P("ch", "ctx"), P("ch"))
    return jax.shard_map(
        body, mesh=mesh, in_specs=placed, out_specs=P(None, ("ctx", "ch")), check_vma=False
    )
```

```python
import jax
import jax.numpy as jnp
import numpy as np
import ml_dtypes
from jax import lax
from jax.experimental import pallas as pl
from jax.experimental.pallas import tpu as pltpu
from jax.sharding import PartitionSpec as P

MESH = pl.DeviceIdType.MESH
F32 = jnp.float32
BF16 = jnp.bfloat16

CTX_Y = 4
CTX = 16
CH = 8
HALF = 8
CHANNELS = 16
BLOCK = 8192
R = 256
Q = 512
GATE_PARTS = 4
PIECE = 1024


def ring(step):
    return min(step, 4 - step)


FAR_FIRST = sorted([(dx, dy) for dx in range(4) for dy in range(4)], key=lambda o: -(ring(o[0]) + ring(o[1])))


COLUMN = ((2, 0), (2, 1), (1, 0), (3, 0), (1, 1), (3, 1), (0, 1))


def pair(table, flip):
    re, im = table.real, table.imag
    return np.block([[re, im], [im, -re]]) if flip else np.block([[re, im], [-im, re]])


def build_tables():
    rows = np.arange(R)
    cols = np.arange(Q)
    part = np.arange(128)
    first = 2 * np.pi * ((np.outer(2 * rows + 1, rows)) % 1024) / 1024.0
    forward = np.concatenate([np.cos(first), -np.sin(first)], axis=0)
    pairs = rows.reshape(CTX, 4, 2, 2)
    order = pairs.transpose(1, 3, 0, 2).reshape(-1)
    backward = np.concatenate([np.cos(first).T, np.sin(first).T], axis=1)[order] * (2.0**-17)
    turn = 2 * np.pi * np.outer(2 * rows + 1, cols) / 2.0**19
    twiddle = np.stack([np.cos(turn), -np.sin(turn)])
    waves = [np.exp(-2j * np.pi * (np.outer(part, d + 4 * part) % Q) / Q) for d in range(4)]
    there = np.concatenate([pair(w, False) for w in waves], axis=0)
    back = np.concatenate([pair(w.T, True) for w in waves], axis=0)
    half = lambda a: a.astype(np.float32).astype(ml_dtypes.bfloat16)
    return half(forward), half(backward), half(there), half(back), twiddle.astype(np.float32)


def times(a, b):
    return a[0] * b[0] - a[1] * b[1], a[0] * b[1] + a[1] * b[0]


def four_point(v):
    (r0, i0), (r1, i1), (r2, i2), (r3, i3) = v
    sr, si, dr, di = r0 + r2, i0 + i2, r0 - r2, i0 - i2
    ur, ui, er, ei = r1 + r3, i1 + i3, r1 - r3, i1 - i3
    return [(sr + ur, si + ui), (dr + ei, di - er), (sr - ur, si - ui), (dr - ei, di + er)]


def kernel(
    pre, val, post, taps, skip_hbm, fwd_t, bwd_t, there_t, back_t, tw_t, y_out, post_out,
    pre_v, val_v, taps_v, fwd_v, bwd_v, there_v, back_v, tw_v,
    sig32, tap32, sig_send, tap_send, sig_recv, tap_recv, skip_send, skip_recv,
    spec_h, y32, direct, lin32, y_send, y_first,
    skip, load_sems, table_sems, sig_sems, tap_sems, pass_sems, skip_sems, post_sems, y_sems, first_sem,
):
    p = lax.axis_index("ctx")
    g = lax.axis_index("ch")
    px, py = p // CTX_Y, p % CTX_Y
    z, core = g // 2, g % 2
    xs = [(px + i) % 4 for i in range(4)]
    ys = [(py + i) % 4 for i in range(4)]
    zs = [(z + i) % 4 for i in range(4)]
    cs = [core, 1 - core]
    sibling = z * 2 + 1 - core
    half = py // 2
    at_home = half == core
    own_group = z * 2 + half
    place = lax.rem(py, 2) * 4 + px
    own_channel = place * 2 + core
    taps_core = p // HALF

    near_y = 2 * core + lax.rem(py, 2)
    flip_y = 2 * core + 1 - lax.rem(py, 2)
    first_y = jnp.where(at_home, flip_y, near_y)
    last_y = jnp.where(at_home, near_y, flip_y)
    workers = [
        (xs[2], first_y), (xs[1], first_y), (xs[3], first_y), (xs[2], last_y),
        (xs[1], last_y), (xs[3], last_y), (xs[0], first_y), (xs[0], last_y),
    ]

    barrier = pltpu.get_barrier_semaphore()
    for dx in (2, 1, 3, 0):
        for dy in (2, 1, 3, 0):
            if dx or dy:
                pl.semaphore_signal(
                    barrier, inc=1, device_id=(xs[dx] * CTX_Y + ys[dy], z * 2 + half), device_id_type=MESH
                )
    for dz, dc in COLUMN:
        pl.semaphore_signal(barrier, inc=1, device_id=(p, zs[dz] * 2 + cs[dc]), device_id_type=MESH)

    loads = [
        pltpu.make_async_copy(a, b, load_sems.at[i])
        for i, (a, b) in enumerate([(taps, taps_v), (pre, pre_v), (val, val_v), (skip_hbm, skip)])
    ]
    tables = [
        pltpu.make_async_copy(a, b, table_sems.at[i])
        for i, (a, b) in enumerate([(fwd_t, fwd_v), (tw_t, tw_v), (there_t, there_v), (back_t, back_v), (bwd_t, bwd_v)])
    ]
    for c in loads + tables:
        c.start()

    loads[0].wait()
    for r in range(16):
        tap32[r : r + 1, :] = taps_v[0:1, r * Q : (r + 1) * Q]
    tap_send[...] = tap32[...].astype(BF16)
    loads[1].wait()
    loads[2].wait()
    for r in range(16):
        at = pl.ds(r * Q, Q)
        prod = pre_v[:, at].astype(F32) * val_v[:, at].astype(F32)
        for q in range(4):
            sig32[q, pl.ds(r, 16, stride=16), :] = prod[:, q * 128 : (q + 1) * 128]
    for q in range(4):
        sig_send[:, :, q * 128 : (q + 1) * 128] = (
            sig32[q].astype(BF16).reshape(CHANNELS, 16, 128)
        )

    @pl.when(at_home)
    def _():
        pl.semaphore_wait(barrier, 7 + 14)

    @pl.when(jnp.logical_not(at_home))
    def _():
        pl.semaphore_wait(barrier, 7 + 16)

    def send_taps(o):
        pltpu.make_async_remote_copy(
            tap_send, tap_recv.at[p], tap_sems.at[0], tap_sems.at[1],
            device_id=(o[0] * CTX_Y + o[1], z * 2 + taps_core), device_id_type=MESH,
        ).start()

    def send_signal(o, k):
        pltpu.make_async_remote_copy(
            sig_send.at[(lax.rem(o[1], 2) * 4 + o[0]) * 2 + k], sig_recv.at[p], sig_sems.at[0], sig_sems.at[1],
            device_id=(o[0] * CTX_Y + o[1], z * 2 + k), device_id_type=MESH,
        ).start()

    for o in workers[:-1]:
        send_taps(o)
    for k in range(2):
        for o in workers[:-1]:
            send_signal(o, k)
    keeps_taps = jnp.logical_and(at_home, taps_core == core)

    @pl.when(keeps_taps)
    def _():
        pltpu.make_async_copy(tap_send, tap_recv.at[p], tap_sems.at[1]).start()

    @pl.when(jnp.logical_not(keeps_taps))
    def _():
        send_taps(workers[-1])

    @pl.when(at_home)
    def _():
        pltpu.make_async_remote_copy(
            sig_send.at[place * 2 + 1 - core], sig_recv.at[p], sig_sems.at[0], sig_sems.at[1],
            device_id=(p, sibling), device_id_type=MESH,
        ).start()
        pltpu.make_async_copy(sig_send.at[own_channel], sig_recv.at[p], sig_sems.at[1]).start()

    @pl.when(jnp.logical_not(at_home))
    def _():
        send_signal(workers[-1], 0)
        send_signal(workers[-1], 1)

    loads[3].wait()
    skip_send[...] = jnp.full((8, 128), skip[place * 2 + 1 - core], F32)
    to_sibling = pltpu.make_async_remote_copy(
        skip_send, skip_recv, skip_sems.at[0], skip_sems.at[1],
        device_id=(p, sibling), device_id_type=MESH,
    )
    to_sibling.start()

    def post_part(o):
        return post.at[:, pl.ds(pl.multiple_of(o * PIECE, PIECE), PIECE)]

    for dz, dc in COLUMN:
        o = zs[dz] * 2 + cs[dc]
        pltpu.make_async_remote_copy(
            post_part(o), post_out.at[g], post_sems.at[0], post_sems.at[1],
            device_id=(p, o), device_id_type=MESH,
        ).start()
    pltpu.make_async_copy(post_part(g), post_out.at[g], post_sems.at[1]).start()

    def lanes(a):
        return slice(a * 128, (a + 1) * 128)

    def turn(a):
        return tw_v[0, :, lanes(a)], tw_v[1, :, lanes(a)]

    def joined(re, im):
        return jnp.concatenate([re.astype(BF16), im.astype(BF16)], axis=1)

    def spectrum(data):
        a = jnp.dot(fwd_v[...], data, preferred_element_type=F32)
        parts = four_point([times((a[:R, lanes(i)], a[R:, lanes(i)]), turn(i)) for i in range(4)])
        return [
            jnp.dot(joined(*parts[d]), there_v[d * R : (d + 1) * R, :], preferred_element_type=F32)
            for d in range(4)
        ]

    def answer(signal):
        for e in range(2):
            for q in range(4):
                direct[pl.ds(e * 4 + q, 128, stride=8), :] = y32[q, pl.ds(e, 128, stride=2), :]
        parts = []
        for d, part in enumerate(spectrum(signal)):
            prod = times((part[:, :128], part[:, 128:]), (spec_h[d, :, :128], spec_h[d, :, 128:]))
            part = jnp.dot(joined(*prod), back_v[d * R : (d + 1) * R, :], preferred_element_type=F32)
            parts.append((part[:, :128], part[:, 128:]))
        parts = [times(part, turn(i)) for i, part in enumerate(four_point(parts))]
        return jnp.concatenate(
            [jnp.concatenate([part[i].astype(BF16) for part in parts], axis=1) for i in range(2)], axis=0
        )

    def pieces(columns, h):
        conv = jnp.dot(bwd_v[h * 64 : (h + 1) * 64], columns, preferred_element_type=F32)
        for e in range(2):
            for q in range(4):
                lin32[h, pl.ds(e * 4 + q, 32, stride=8), :] = conv[e * 32 : (e + 1) * 32, lanes(q)]
        total = lin32[h].reshape(CTX, 16, 128) + direct[...].reshape(CTX, 4, 16, 128)[:, h]
        return total.reshape(CTX, 2, 8, 128).astype(BF16)

    for c in tables:
        c.wait()

    @pl.when(p == 0)
    def _():
        gap = jnp.zeros((16, Q), BF16)
        first = jnp.concatenate([tap_send[...], jnp.zeros((R - 16, Q), BF16)], axis=0)
        for d, part in enumerate(spectrum(first)):
            spec_h[d] = part

        def eight_channels(r, carry):
            rows = []
            for i in range(8):
                own = sig_send[r * 8 + i]
                rows += [own, gap]
                for q in range(4):
                    y32[q, 32 * i : 32 * i + 16, :] = skip[r * 8 + i] * own[:, lanes(q)].astype(F32)
                    y32[q, 32 * i + 16 : 32 * i + 32, :] = jnp.zeros((16, 128), F32)
            columns = answer(jnp.concatenate(rows, axis=0))
            for h in range(4):
                part = pieces(columns, h).reshape(8, 2, 2, 8, 128)
                for k in range(2):
                    y_first[r, :, k * 8 + 2 * h : k * 8 + 2 * h + 2] = part[:, k]
            to = pl.ds(g * CHANNELS + r * 8, 8)
            for dz, dc in COLUMN:
                o = zs[dz] * 2 + cs[dc]
                pltpu.make_async_remote_copy(
                    y_first.at[r, :, o], y_out.at[to], first_sem, y_sems.at[1],
                    device_id=(p, o), device_id_type=MESH,
                ).start()
            pltpu.make_async_copy(y_first.at[r, :, g], y_out.at[to], y_sems.at[1]).start()
            return carry

        lax.fori_loop(0, 2, eight_channels, 0)

    mine = tap_recv.at[pl.ds(core * HALF, HALF)]
    theirs = tap_recv.at[pl.ds((1 - core) * HALF, HALF)]
    pltpu.make_async_copy(mine, mine, tap_sems.at[1]).wait()
    passed = pltpu.make_async_remote_copy(
        mine, mine, pass_sems.at[0], pass_sems.at[1], device_id=(p, sibling), device_id_type=MESH
    )
    passed.start()

    pltpu.make_async_copy(theirs, theirs, pass_sems.at[1]).wait()
    for d, part in enumerate(spectrum(tap_recv[...].reshape(R, Q))):
        spec_h[d] = part

    pltpu.make_async_copy(sig_recv, sig_recv, sig_sems.at[1]).wait()
    signal = sig_recv[...].reshape(R, Q)
    to_sibling.wait_recv()
    weight = jnp.where(at_home, skip[own_channel], skip_recv[0:1, :])
    for q in range(4):
        y32[q] = weight * signal[:, lanes(q)].astype(F32)
    columns = answer(signal)

    channel = own_group * CHANNELS + own_channel
    def send_piece(o_ctx, o_ch):
        pltpu.make_async_remote_copy(
            y_send.at[o_ctx, o_ch], y_out.at[channel], y_sems.at[0], y_sems.at[1],
            device_id=(o_ctx, o_ch), device_id_type=MESH,
        ).start()

    for o_z in range(4):
        y_send[:, o_z * 2 : o_z * 2 + 2] = pieces(columns, o_z)
        for c, (dx, dy) in [(c, o) for c in range(2) for o in FAR_FIRST]:
            o_ctx = xs[dx] * CTX_Y + ys[dy]

            @pl.when(o_ctx != 0)
            def _(o_ctx=o_ctx, o_z=o_z, c=c, same=not (dx or dy)):
                if same:

                    @pl.when(g != o_z * 2 + c)
                    def _():
                        send_piece(o_ctx, o_z * 2 + c)

                else:
                    send_piece(o_ctx, o_z * 2 + c)

    @pl.when(p != 0)
    def _():
        pltpu.make_async_copy(y_send.at[p, g], y_out.at[channel], y_sems.at[1]).start()

    @pl.when(at_home)
    def _():
        part = sig_send.at[pl.ds(0, 15)]
        pltpu.make_async_copy(part, part, sig_sems.at[0]).wait()

    @pl.when(jnp.logical_not(at_home))
    def _():
        pltpu.make_async_copy(sig_send, sig_send, sig_sems.at[0]).wait()

    @pl.when(keeps_taps)
    def _():
        part = tap_recv.at[pl.ds(0, 7)]
        pltpu.make_async_copy(part, part, tap_sems.at[0]).wait()

    @pl.when(jnp.logical_not(keeps_taps))
    def _():
        part = tap_recv.at[pl.ds(0, 8)]
        pltpu.make_async_copy(part, part, tap_sems.at[0]).wait()

    passed.wait_send()
    to_sibling.wait_send()
    part = post_out.at[pl.ds(0, CH - 1)]
    pltpu.make_async_copy(part, part, post_sems.at[0]).wait()
    pltpu.make_async_copy(post_out, post_out, post_sems.at[1]).wait()

    @pl.when(p == 0)
    def _():
        part = y_out.at[pl.ds(0, (CTX - 1) * CH)]
        pltpu.make_async_copy(part, part, y_sems.at[0]).wait()
        part = y_out.at[pl.ds(0, 2 * 8 * (CH - 1))]
        pltpu.make_async_copy(part, part, first_sem).wait()

    @pl.when(p != 0)
    def _():
        part = y_out.at[pl.ds(0, (CTX - 1) * CH - 1)]
        pltpu.make_async_copy(part, part, y_sems.at[0]).wait()

    pltpu.make_async_copy(y_out, y_out, y_sems.at[1]).wait()


def gate_kernel(y, post, out, wide, made, sems):
    rows = CTX * CH // GATE_PARTS
    copies = []
    for k in range(GATE_PARTS):
        own = pl.ds(k * rows, rows)
        wide[k] = y[own].astype(F32).reshape(rows * 8, 128)
        for s in range(8):
            at = pl.ds(s * 128, 128)
            gate = post[own, at].astype(F32)
            made[own, at] = (wide[k, pl.ds(s, rows, stride=8), :] * gate).astype(BF16)
        copies.append(pltpu.make_async_copy(made.at[own], out.at[own], sems.at[k]))
        copies[-1].start()
    for copy in copies:
        copy.wait()


def body(pre_gate, value, post_gate, filter_taps, skip):
    tables = tuple(jnp.asarray(t) for t in build_tables())
    anyspace = pl.BlockSpec(memory_space=pl.ANY)
    vmem = pltpu.VMEM
    dma = pltpu.SemaphoreType.DMA
    whole = pl.BlockSpec(memory_space=vmem)
    conv, gate = pl.pallas_call(
        kernel,
        out_shape=[
            vmem((CTX * CH, 8, 128), BF16),
            vmem((CH, CHANNELS, PIECE), BF16),
        ],
        in_specs=[anyspace] * 10,
        out_specs=[whole, whole],
        scratch_shapes=[
            vmem((CHANNELS, BLOCK), BF16),
            vmem((CHANNELS, BLOCK), BF16),
            vmem((1, BLOCK), F32),
            vmem((2 * R, R), BF16),
            vmem((R, 2 * R), BF16),
            vmem((4 * R, R), BF16),
            vmem((4 * R, R), BF16),
            vmem((2, R, Q), F32),
            vmem((4, R, 128), F32),
            vmem((16, Q), F32),
            vmem((CTX, 16, Q), BF16),
            vmem((16, Q), BF16),
            vmem((CTX, 16, Q), BF16),
            vmem((CTX, 16, Q), BF16),
            vmem((8, 128), F32),
            vmem((8, 128), F32),
            vmem((4, R, 2 * 128), F32),
            vmem((4, R, 128), F32),
            vmem((CTX * CH * 8, 128), F32),
            vmem((4, CTX * CH * 2, 128), F32),
            vmem((CTX, CH, 8, 128), BF16),
            vmem((2, 8, 16, 8, 128), BF16),
            pltpu.SMEM((16,), F32),
            dma((4,)),
            dma((5,)),
            dma((2,)),
            dma((2,)),
            dma((2,)),
            dma((2,)),
            dma((2,)),
            dma((2,)),
            dma,
        ],
        compiler_params=pltpu.CompilerParams(
            collective_id=0, has_side_effects=True, vmem_limit_bytes=56 * 1024 * 1024
        ),
        name="hyena",
    )(pre_gate, value, post_gate, filter_taps, skip, *tables)
    return pl.pallas_call(
        gate_kernel,
        out_shape=jax.ShapeDtypeStruct((CTX * CH, PIECE), BF16),
        in_specs=[whole, whole],
        out_specs=anyspace,
        scratch_shapes=[
            vmem((GATE_PARTS, CTX * CH * 8 // GATE_PARTS, 128), F32),
            vmem((CTX * CH, PIECE), BF16),
            dma((GATE_PARTS,)),
        ],
        compiler_params=pltpu.CompilerParams(vmem_limit_bytes=4 * 1024 * 1024),
        name="gate",
    )(conv, gate.reshape(CTX * CH, PIECE))


def solution(mesh):
    placed = (P("ch", "ctx"), P("ch", "ctx"), P("ch", "ctx"), P("ch", "ctx"), P("ch"))
    return jax.shard_map(
        body, mesh=mesh, in_specs=placed, out_specs=P(None, ("ctx", "ch")), check_vma=False
    )
```

```python
import jax
import jax.numpy as jnp
import numpy as np
import ml_dtypes
from jax import lax
from jax.experimental import pallas as pl
from jax.experimental.pallas import tpu as pltpu
from jax.sharding import PartitionSpec as P

MESH = pl.DeviceIdType.MESH
F32 = jnp.float32
BF16 = jnp.bfloat16

CTX_Y = 4
CTX = 16
CH = 8
HALF = 8
CHANNELS = 16
BLOCK = 8192
R = 256
Q = 512
GATE_PARTS = 4
PIECE = 1024


def ring(step):
    return min(step, 4 - step)


FAR_FIRST = sorted([(dx, dy) for dx in range(4) for dy in range(4)], key=lambda o: -(ring(o[0]) + ring(o[1])))


COLUMN = ((2, 0), (2, 1), (1, 0), (3, 0), (1, 1), (3, 1), (0, 1))


def pair(table, flip):
    re, im = table.real, table.imag
    return np.block([[re, im], [im, -re]]) if flip else np.block([[re, im], [-im, re]])


def build_tables():
    rows = np.arange(R)
    cols = np.arange(Q)
    part = np.arange(128)
    first = 2 * np.pi * ((np.outer(2 * rows + 1, rows)) % 1024) / 1024.0
    forward = np.concatenate([np.cos(first), -np.sin(first)], axis=0)
    pairs = rows.reshape(CTX, 2, 4, 2)
    order = pairs.transpose(1, 3, 0, 2).reshape(-1)
    backward = np.concatenate([np.cos(first).T, np.sin(first).T], axis=1)[order] * (2.0**-17)
    turn = 2 * np.pi * np.outer(2 * rows + 1, cols) / 2.0**19
    twiddle = np.stack([np.cos(turn), -np.sin(turn)])
    waves = [np.exp(-2j * np.pi * (np.outer(part, d + 4 * part) % Q) / Q) for d in range(4)]
    there = np.concatenate([pair(w, False) for w in waves], axis=0)
    back = np.concatenate([pair(w.T, True) for w in waves], axis=0)
    half = lambda a: a.astype(np.float32).astype(ml_dtypes.bfloat16)
    return half(forward), half(backward), half(there), half(back), twiddle.astype(np.float32)


def times(a, b):
    return a[0] * b[0] - a[1] * b[1], a[0] * b[1] + a[1] * b[0]


def four_point(v):
    (r0, i0), (r1, i1), (r2, i2), (r3, i3) = v
    sr, si, dr, di = r0 + r2, i0 + i2, r0 - r2, i0 - i2
    ur, ui, er, ei = r1 + r3, i1 + i3, r1 - r3, i1 - i3
    return [(sr + ur, si + ui), (dr + ei, di - er), (sr - ur, si - ui), (dr - ei, di + er)]


def kernel(
    pre, val, post, taps, skip_hbm, fwd_t, bwd_t, there_t, back_t, tw_t, y_out, post_out,
    pre_v, val_v, taps_v, fwd_v, bwd_v, there_v, back_v, tw_v,
    sig32, tap32, sig_send, tap_send, sig_recv, tap_recv, skip_send, skip_recv,
    spec_h, y32, direct, lin32, y_send, y_first,
    skip, load_sems, table_sems, sig_sems, tap_sems, pass_sems, skip_sems, post_sems, y_sems, first_sem,
):
    p = lax.axis_index("ctx")
    g = lax.axis_index("ch")
    px, py = p // CTX_Y, p % CTX_Y
    z, core = g // 2, g % 2
    xs = [(px + i) % 4 for i in range(4)]
    ys = [(py + i) % 4 for i in range(4)]
    zs = [(z + i) % 4 for i in range(4)]
    cs = [core, 1 - core]
    sibling = z * 2 + 1 - core
    half = py // 2
    at_home = half == core
    own_group = z * 2 + half
    place = lax.rem(py, 2) * 4 + px
    own_channel = place * 2 + core
    taps_core = p // HALF

    near_y = 2 * core + lax.rem(py, 2)
    flip_y = 2 * core + 1 - lax.rem(py, 2)
    first_y = jnp.where(at_home, flip_y, near_y)
    last_y = jnp.where(at_home, near_y, flip_y)
    workers = [
        (xs[2], first_y), (xs[1], first_y), (xs[3], first_y), (xs[2], last_y),
        (xs[1], last_y), (xs[3], last_y), (xs[0], first_y), (xs[0], last_y),
    ]

    barrier = pltpu.get_barrier_semaphore()
    for dx in (2, 1, 3, 0):
        for dy in (2, 1, 3, 0):
            if dx or dy:
                pl.semaphore_signal(
                    barrier, inc=1, device_id=(xs[dx] * CTX_Y + ys[dy], z * 2 + half), device_id_type=MESH
                )
    for dz, dc in COLUMN:
        pl.semaphore_signal(barrier, inc=1, device_id=(p, zs[dz] * 2 + cs[dc]), device_id_type=MESH)

    loads = [
        pltpu.make_async_copy(a, b, load_sems.at[i])
        for i, (a, b) in enumerate([(taps, taps_v), (pre, pre_v), (val, val_v), (skip_hbm, skip)])
    ]
    tables = [
        pltpu.make_async_copy(a, b, table_sems.at[i])
        for i, (a, b) in enumerate([(fwd_t, fwd_v), (tw_t, tw_v), (there_t, there_v), (back_t, back_v), (bwd_t, bwd_v)])
    ]
    for c in loads + tables:
        c.start()

    loads[0].wait()
    for r in range(16):
        tap32[r : r + 1, :] = taps_v[0:1, r * Q : (r + 1) * Q]
    tap_send[...] = tap32[...].astype(BF16)
    loads[1].wait()
    loads[2].wait()
    for r in range(16):
        at = pl.ds(r * Q, Q)
        prod = pre_v[:, at].astype(F32) * val_v[:, at].astype(F32)
        for q in range(4):
            sig32[q, pl.ds(r, 16, stride=16), :] = prod[:, q * 128 : (q + 1) * 128]
    for q in range(4):
        sig_send[:, :, q * 128 : (q + 1) * 128] = (
            sig32[q].astype(BF16).reshape(CHANNELS, 16, 128)
        )

    @pl.when(at_home)
    def _():
        pl.semaphore_wait(barrier, 7 + 14)

    @pl.when(jnp.logical_not(at_home))
    def _():
        pl.semaphore_wait(barrier, 7 + 16)

    def send_taps(o):
        pltpu.make_async_remote_copy(
            tap_send, tap_recv.at[p], tap_sems.at[0], tap_sems.at[1],
            device_id=(o[0] * CTX_Y + o[1], z * 2 + taps_core), device_id_type=MESH,
        ).start()

    def send_signal(o, k):
        pltpu.make_async_remote_copy(
            sig_send.at[(lax.rem(o[1], 2) * 4 + o[0]) * 2 + k], sig_recv.at[p], sig_sems.at[0], sig_sems.at[1],
            device_id=(o[0] * CTX_Y + o[1], z * 2 + k), device_id_type=MESH,
        ).start()

    for o in workers[:-1]:
        send_taps(o)
    for k in range(2):
        for o in workers[:-1]:
            send_signal(o, k)
    keeps_taps = jnp.logical_and(at_home, taps_core == core)

    @pl.when(keeps_taps)
    def _():
        pltpu.make_async_copy(tap_send, tap_recv.at[p], tap_sems.at[1]).start()

    @pl.when(jnp.logical_not(keeps_taps))
    def _():
        send_taps(workers[-1])

    @pl.when(at_home)
    def _():
        pltpu.make_async_remote_copy(
            sig_send.at[place * 2 + 1 - core], sig_recv.at[p], sig_sems.at[0], sig_sems.at[1],
            device_id=(p, sibling), device_id_type=MESH,
        ).start()
        pltpu.make_async_copy(sig_send.at[own_channel], sig_recv.at[p], sig_sems.at[1]).start()

    @pl.when(jnp.logical_not(at_home))
    def _():
        send_signal(workers[-1], 0)
        send_signal(workers[-1], 1)

    loads[3].wait()
    skip_send[...] = jnp.full((8, 128), skip[place * 2 + 1 - core], F32)
    to_sibling = pltpu.make_async_remote_copy(
        skip_send, skip_recv, skip_sems.at[0], skip_sems.at[1],
        device_id=(p, sibling), device_id_type=MESH,
    )
    to_sibling.start()

    def post_part(o):
        return post.at[:, pl.ds(pl.multiple_of(o * PIECE, PIECE), PIECE)]

    for dz, dc in COLUMN:
        o = zs[dz] * 2 + cs[dc]
        pltpu.make_async_remote_copy(
            post_part(o), post_out.at[g], post_sems.at[0], post_sems.at[1],
            device_id=(p, o), device_id_type=MESH,
        ).start()
    pltpu.make_async_copy(post_part(g), post_out.at[g], post_sems.at[1]).start()

    def lanes(a):
        return slice(a * 128, (a + 1) * 128)

    def turn(a):
        return tw_v[0, :, lanes(a)], tw_v[1, :, lanes(a)]

    def joined(re, im):
        return jnp.concatenate([re.astype(BF16), im.astype(BF16)], axis=1)

    def spectrum(data):
        a = jnp.dot(fwd_v[...], data, preferred_element_type=F32)
        parts = four_point([times((a[:R, lanes(i)], a[R:, lanes(i)]), turn(i)) for i in range(4)])
        return [
            jnp.dot(joined(*parts[d]), there_v[d * R : (d + 1) * R, :], preferred_element_type=F32)
            for d in range(4)
        ]

    def answer(signal):
        for e in range(2):
            for q in range(4):
                direct[pl.ds(e * 4 + q, 128, stride=8), :] = y32[q, pl.ds(e, 128, stride=2), :]
        parts = []
        for d, part in enumerate(spectrum(signal)):
            prod = times((part[:, :128], part[:, 128:]), (spec_h[d, :, :128], spec_h[d, :, 128:]))
            part = jnp.dot(joined(*prod), back_v[d * R : (d + 1) * R, :], preferred_element_type=F32)
            parts.append((part[:, :128], part[:, 128:]))
        parts = [times(part, turn(i)) for i, part in enumerate(four_point(parts))]
        return jnp.concatenate(
            [jnp.concatenate([part[i].astype(BF16) for part in parts], axis=1) for i in range(2)], axis=0
        )

    def pieces(columns, h):
        conv = jnp.dot(bwd_v[h * 128 : (h + 1) * 128], columns, preferred_element_type=F32)
        for e in range(2):
            for q in range(4):
                lin32[h, pl.ds(e * 4 + q, 64, stride=8), :] = conv[e * 64 : (e + 1) * 64, lanes(q)]
        total = lin32[h].reshape(CTX, 32, 128) + direct[...].reshape(CTX, 2, 32, 128)[:, h]
        return total.reshape(CTX, 4, 8, 128).astype(BF16)

    for c in tables:
        c.wait()

    @pl.when(p == 0)
    def _():
        gap = jnp.zeros((16, Q), BF16)
        first = jnp.concatenate([tap_send[...], jnp.zeros((R - 16, Q), BF16)], axis=0)
        for d, part in enumerate(spectrum(first)):
            spec_h[d] = part

        def eight_channels(r, carry):
            rows = []
            for i in range(8):
                own = sig_send[r * 8 + i]
                rows += [own, gap]
                for q in range(4):
                    y32[q, 32 * i : 32 * i + 16, :] = skip[r * 8 + i] * own[:, lanes(q)].astype(F32)
                    y32[q, 32 * i + 16 : 32 * i + 32, :] = jnp.zeros((16, 128), F32)
            columns = answer(jnp.concatenate(rows, axis=0))
            for h in range(2):
                part = pieces(columns, h).reshape(8, 2, 4, 8, 128)
                for k in range(2):
                    y_first[r, :, k * 8 + 4 * h : k * 8 + 4 * h + 4] = part[:, k]
            to = pl.ds(g * CHANNELS + r * 8, 8)
            for dz, dc in COLUMN:
                o = zs[dz] * 2 + cs[dc]
                pltpu.make_async_remote_copy(
                    y_first.at[r, :, o], y_out.at[to], first_sem, y_sems.at[1],
                    device_id=(p, o), device_id_type=MESH,
                ).start()
            pltpu.make_async_copy(y_first.at[r, :, g], y_out.at[to], y_sems.at[1]).start()
            return carry

        lax.fori_loop(0, 2, eight_channels, 0)

    mine = tap_recv.at[pl.ds(core * HALF, HALF)]
    theirs = tap_recv.at[pl.ds((1 - core) * HALF, HALF)]
    pltpu.make_async_copy(mine, mine, tap_sems.at[1]).wait()
    passed = pltpu.make_async_remote_copy(
        mine, mine, pass_sems.at[0], pass_sems.at[1], device_id=(p, sibling), device_id_type=MESH
    )
    passed.start()

    pltpu.make_async_copy(theirs, theirs, pass_sems.at[1]).wait()
    for d, part in enumerate(spectrum(tap_recv[...].reshape(R, Q))):
        spec_h[d] = part

    pltpu.make_async_copy(sig_recv, sig_recv, sig_sems.at[1]).wait()
    signal = sig_recv[...].reshape(R, Q)
    to_sibling.wait_recv()
    weight = jnp.where(at_home, skip[own_channel], skip_recv[0:1, :])
    for q in range(4):
        y32[q] = weight * signal[:, lanes(q)].astype(F32)
    columns = answer(signal)

    channel = own_group * CHANNELS + own_channel
    def send_piece(o_ctx, o_ch):
        pltpu.make_async_remote_copy(
            y_send.at[o_ctx, o_ch], y_out.at[channel], y_sems.at[0], y_sems.at[1],
            device_id=(o_ctx, o_ch), device_id_type=MESH,
        ).start()

    for o_z in range(4):
        if o_z % 2 == 0:
            y_send[:, o_z * 2 : o_z * 2 + 4] = pieces(columns, o_z // 2)
        for dx, dy in FAR_FIRST:
            o_ctx = xs[dx] * CTX_Y + ys[dy]

            @pl.when(o_ctx != 0)
            def _(o_ctx=o_ctx, o_z=o_z, same=not (dx or dy)):
                for c in (1, 0):
                    if same:

                        @pl.when(g != o_z * 2 + c)
                        def _(c=c):
                            send_piece(o_ctx, o_z * 2 + c)

                    else:
                        send_piece(o_ctx, o_z * 2 + c)

    @pl.when(p != 0)
    def _():
        pltpu.make_async_copy(y_send.at[p, g], y_out.at[channel], y_sems.at[1]).start()

    @pl.when(at_home)
    def _():
        part = sig_send.at[pl.ds(0, 15)]
        pltpu.make_async_copy(part, part, sig_sems.at[0]).wait()

    @pl.when(jnp.logical_not(at_home))
    def _():
        pltpu.make_async_copy(sig_send, sig_send, sig_sems.at[0]).wait()

    @pl.when(keeps_taps)
    def _():
        part = tap_recv.at[pl.ds(0, 7)]
        pltpu.make_async_copy(part, part, tap_sems.at[0]).wait()

    @pl.when(jnp.logical_not(keeps_taps))
    def _():
        part = tap_recv.at[pl.ds(0, 8)]
        pltpu.make_async_copy(part, part, tap_sems.at[0]).wait()

    passed.wait_send()
    to_sibling.wait_send()
    part = post_out.at[pl.ds(0, CH - 1)]
    pltpu.make_async_copy(part, part, post_sems.at[0]).wait()
    pltpu.make_async_copy(post_out, post_out, post_sems.at[1]).wait()

    @pl.when(p == 0)
    def _():
        part = y_out.at[pl.ds(0, (CTX - 1) * CH)]
        pltpu.make_async_copy(part, part, y_sems.at[0]).wait()
        part = y_out.at[pl.ds(0, 2 * 8 * (CH - 1))]
        pltpu.make_async_copy(part, part, first_sem).wait()

    @pl.when(p != 0)
    def _():
        part = y_out.at[pl.ds(0, (CTX - 1) * CH - 1)]
        pltpu.make_async_copy(part, part, y_sems.at[0]).wait()

    pltpu.make_async_copy(y_out, y_out, y_sems.at[1]).wait()


def gate_kernel(y, post, out, wide, made, sems):
    rows = CTX * CH // GATE_PARTS
    copies = []
    for k in range(GATE_PARTS):
        own = pl.ds(k * rows, rows)
        wide[k] = y[own].astype(F32).reshape(rows * 8, 128)
        for s in range(8):
            at = pl.ds(s * 128, 128)
            gate = post[own, at].astype(F32)
            made[own, at] = (wide[k, pl.ds(s, rows, stride=8), :] * gate).astype(BF16)
        copies.append(pltpu.make_async_copy(made.at[own], out.at[own], sems.at[k]))
        copies[-1].start()
    for copy in copies:
        copy.wait()


def body(pre_gate, value, post_gate, filter_taps, skip):
    tables = tuple(jnp.asarray(t) for t in build_tables())
    anyspace = pl.BlockSpec(memory_space=pl.ANY)
    vmem = pltpu.VMEM
    dma = pltpu.SemaphoreType.DMA
    whole = pl.BlockSpec(memory_space=vmem)
    conv, gate = pl.pallas_call(
        kernel,
        out_shape=[
            vmem((CTX * CH, 8, 128), BF16),
            vmem((CH, CHANNELS, PIECE), BF16),
        ],
        in_specs=[anyspace] * 10,
        out_specs=[whole, whole],
        scratch_shapes=[
            vmem((CHANNELS, BLOCK), BF16),
            vmem((CHANNELS, BLOCK), BF16),
            vmem((1, BLOCK), F32),
            vmem((2 * R, R), BF16),
            vmem((R, 2 * R), BF16),
            vmem((4 * R, R), BF16),
            vmem((4 * R, R), BF16),
            vmem((2, R, Q), F32),
            vmem((4, R, 128), F32),
            vmem((16, Q), F32),
            vmem((CTX, 16, Q), BF16),
            vmem((16, Q), BF16),
            vmem((CTX, 16, Q), BF16),
            vmem((CTX, 16, Q), BF16),
            vmem((8, 128), F32),
            vmem((8, 128), F32),
            vmem((4, R, 2 * 128), F32),
            vmem((4, R, 128), F32),
            vmem((CTX * CH * 8, 128), F32),
            vmem((2, CTX * CH * 4, 128), F32),
            vmem((CTX, CH, 8, 128), BF16),
            vmem((2, 8, 16, 8, 128), BF16),
            pltpu.SMEM((16,), F32),
            dma((4,)),
            dma((5,)),
            dma((2,)),
            dma((2,)),
            dma((2,)),
            dma((2,)),
            dma((2,)),
            dma((2,)),
            dma,
        ],
        compiler_params=pltpu.CompilerParams(
            collective_id=0, has_side_effects=True, vmem_limit_bytes=56 * 1024 * 1024
        ),
        name="hyena",
    )(pre_gate, value, post_gate, filter_taps, skip, *tables)
    return pl.pallas_call(
        gate_kernel,
        out_shape=jax.ShapeDtypeStruct((CTX * CH, PIECE), BF16),
        in_specs=[whole, whole],
        out_specs=anyspace,
        scratch_shapes=[
            vmem((GATE_PARTS, CTX * CH * 8 // GATE_PARTS, 128), F32),
            vmem((CTX * CH, PIECE), BF16),
            dma((GATE_PARTS,)),
        ],
        compiler_params=pltpu.CompilerParams(vmem_limit_bytes=4 * 1024 * 1024),
        name="gate",
    )(conv, gate.reshape(CTX * CH, PIECE))


def solution(mesh):
    placed = (P("ch", "ctx"), P("ch", "ctx"), P("ch", "ctx"), P("ch", "ctx"), P("ch"))
    return jax.shard_map(
        body, mesh=mesh, in_specs=placed, out_specs=P(None, ("ctx", "ch")), check_vma=False
    )
```
